128 devices in a mesh: row: 16 (over x, z_lo, core), col: 8 (over y, z_hi).
Axes of the slice: x: 4, y: 4, z: 4 (z_hi: 2, z_lo: 2; z = z_hi * 2 + z_lo), core: 2. Of those that a mesh axis runs over, the one named last changes fastest.
Arguments:
- volume: bfloat16 [512, 8192], P('row', 'col'), may hold values from -6 to 6
- filters: bfloat16 [27, 512, 512], P(None, 'row', 'col'), may hold values from -0.0546875 to 0.0546875
- bias: bfloat16 [512], P('col'), may hold values from -3 to 3
- cotangent: bfloat16 [512, 8192], P('row', 'col'), may hold values from -6 to 6
Outputs:
- output: bfloat16 [512, 8192], P('row', 'col')
- data_grad: bfloat16 [512, 8192], P('row', 'col')
- weight_grad: float32 [27, 512, 512], P(None, 'row', 'col')
- bias_grad: float32 [512], P('row')
The draws below stay inside these ranges and needn't reach their ends.
All inputs are finite; a program needn't handle non-finite values.
Results may differ from the reference program's by a relative error of at most 0.0075.
Values may be sent and summed in bfloat16 or wider, within the bound.
A program may use at most 192 MiB of HBM per device.

```python
import jax
import jax.numpy as jnp
from jax import lax

C = 512
F = 512
S = 32
NX = 8
NVOX = 8192


def level_of(stream_key, shape, shards, least, top_value):
    factor_of, own = 1.0, jax.random.fold_in(stream_key, 6)
    for position, shards_of in shards:
        steps = jnp.exp(jax.random.uniform(jax.random.fold_in(own, position), (shards_of,), jnp.float32, least / len(shards), top_value / len(shards)))
        factor_of = factor_of * jnp.repeat(steps, shape[position] // shards_of).reshape([-1 if axis == position else 1 for axis in range(len(shape))])
    return factor_of


def noise(own_key, shape, scale, reach, pieces=(), kind=jnp.bfloat16):
    factor_of = level_of(own_key, shape, pieces, -0.22, 0.18) if pieces else 1.0
    drawn = jax.random.normal(own_key, shape, jnp.float32) * scale * factor_of
    return jnp.minimum(jnp.maximum(drawn, -reach), reach).astype(kind)


def setup_inputs(seed: int = 0) -> dict:
    streams_of = jax.random.split(jax.random.key(seed), 5)
    return {
        "volume": noise(streams_of[0], (C, NVOX), 1.0, 6.0, ((0, 16), (1, 8))),
        "filters": noise(streams_of[1], (27, C, F), (27 * C) ** -0.5, 0.0546875, ((1, 16), (2, 8))),
        "bias": noise(streams_of[2], (F,), 0.5, 3.0, ((0, 8),)),
        "cotangent": noise(streams_of[3], (F, NVOX), 1.0, 6.0, ((0, 16), (1, 8))),
    }


def silu_slope(value):
    logistic = jax.nn.sigmoid(value)
    return logistic * (1.0 + value * (1.0 - logistic))

def tap_view(padded, tap_index, planes, flipped):
    depth = tap_index // 9
    height = tap_index // 3 % 3
    across = tap_index % 3
    if flipped:
        depth, height, across = (2 - depth, 2 - height, 2 - across)
    side = padded.shape[3] - 2
    piece = padded[:, depth:depth + planes, height:height + side, across:across + side]
    return piece.reshape(padded.shape[0], planes * side * side)

def reference(volume, filters, bias, cotangent):
    norm_factor = 1.0 / jnp.sqrt(jnp.float32(NVOX))
    padded = jnp.pad(volume.reshape(C, NX, S, S), ((0, 0), (1, 1), (1, 1), (1, 1)))
    sectioned = jnp.zeros((F, NVOX), jnp.float32)
    for tap_index in range(27):
        view = tap_view(padded, tap_index, NX, False).astype(jnp.float32)
        sectioned = sectioned + jnp.dot(filters[tap_index].astype(jnp.float32).T, view)
    sectioned = sectioned + bias.astype(jnp.float32)[:, None]
    output = jax.nn.silu(sectioned).astype(jnp.bfloat16)
    slope_grad = (cotangent.astype(jnp.float32) * silu_slope(sectioned)).astype(jnp.bfloat16)
    grad_wide = slope_grad.astype(jnp.float32)
    bias_grad = lax.optimization_barrier(jnp.sum(grad_wide, axis=1)) * norm_factor
    weight_terms = []
    for tap_index in range(27):
        view = tap_view(padded, tap_index, NX, False).astype(jnp.float32)
        weight_terms.append(jnp.dot(view, grad_wide.T))
    weight_grad = jnp.stack(weight_terms) * norm_factor
    grad_padded = jnp.pad(grad_wide.reshape(F, NX, S, S), ((0, 0), (1, 1), (1, 1), (1, 1)))
    data_sum = jnp.zeros((C, NVOX), jnp.float32)
    for tap_index in range(27):
        view = tap_view(grad_padded, tap_index, NX, True)
        data_sum = data_sum + jnp.dot(filters[tap_index].astype(jnp.float32), view)
    return (output, data_sum.astype(jnp.bfloat16), weight_grad, bias_grad)
```

```python
import functools
import math

import jax
import jax.numpy as jnp
from jax import lax
from jax.experimental import pallas as pl
from jax.experimental.pallas import tpu as pltpu
from jax.sharding import PartitionSpec as P

S = 32
VOX = S * S
CH = 32
TAPS = 27
DEPTH = TAPS * CH
PADDED = 896
MESH = pl.DeviceIdType.MESH
BF16 = jnp.bfloat16
F32 = jnp.float32


def positions():
    lane = lax.broadcasted_iota(jnp.int32, (CH, VOX), 1)
    return lane // S, lane % S


def inside(coord, step):
    moved = coord + step
    return (moved >= 0) & (moved < S)


def moved_view(value, y, x, dy, dx):
    offset = dy * S + dx
    if offset:
        value = pltpu.roll(value, (-offset) % VOX, 1)
    if dy or dx:
        keep = inside(y, dy) & inside(x, dx)
        value = jnp.where(keep, value, 0.0)
    return value


def kernel(
    nc, norm_factor,
    vol_ref, w_ref, bias_ref, cot_ref,
    out_ref, dgrad_ref, wgrad_ref, bgrad_ref,
    wpad, wt_own, wg, xin, xcol, ypart, yrecv, g, wgp, wgrecv, bsend, brecv, z, dsend, dacc, drecv,
    x_send, x_recv, w_send, w_recv, y_send, y_recv, g_send, g_recv, b_send, b_recv, wg_send, wg_recv, d_send, d_recv,
):
    row = lax.axis_index("row")
    col = lax.axis_index("col")
    q = row // 2
    k = row % 2
    sib = 2 * q + 1 - k
    up = (col + 1) % nc
    down = (col + nc - 1) % nc

    def rows(start, size=CH):
        return pl.ds(pl.multiple_of(start, CH), size)

    def send(src, dst, send_sem, recv_sem, to_row, to_col):
        copy = pltpu.make_async_remote_copy(
            src_ref=src, dst_ref=dst, send_sem=send_sem, recv_sem=recv_sem,
            device_id=(to_row, to_col), device_id_type=MESH,
        )
        copy.start()
        return copy

    barrier = pltpu.get_barrier_semaphore()
    for d in range(nc):
        for o in range(2):
            if d or o:
                pl.semaphore_signal(
                    barrier, inc=1, device_id=(sib if o else row, (col + d) % nc), device_id_type=MESH
                )
    for j in range(1, nc):
        pl.semaphore_signal(
            barrier, inc=1, device_id=(2 * ((q + j) % nc) + k, col), device_id_type=MESH
        )

    wpad[...] = jnp.zeros_like(wpad)
    wpad[0:DEPTH, 0 : 2 * CH] = w_ref[...].reshape(DEPTH, 2 * CH).astype(F32)
    wpad[DEPTH : DEPTH + 1, 0 : 2 * CH] = bias_ref[...].astype(F32)
    wt_own[...] = jnp.transpose(wpad[...])[0 : 2 * CH].astype(BF16)
    xin[1, rows(CH * k), :] = vol_ref[...]
    bsend[...] = jnp.zeros_like(bsend)

    pl.semaphore_wait(barrier, 3 * nc - 2)

    copies = []
    x_copies = {}
    for a, to_col in ((1, col), (0, up), (2, down)):
        for o in range(2):
            if a == 1 and o == 0:
                continue
            x_copies[a, o] = send(
                vol_ref, xin.at[a, rows(CH * k), :], x_send.at[a, o], x_recv.at[a, o],
                sib if o else row, to_col,
            )
    w_copies = {}
    for d in range(nc):
        for o in range(2):
            half = 1 - k if o else k
            if d == 0 and o == 0:
                wg[k, 0:CH, :] = wt_own[rows(CH * k), :]
                continue
            w_copies[d, o] = send(
                wt_own.at[rows(CH * half), :], wg.at[k, pl.ds(CH * d, CH), :],
                w_send.at[d, o], w_recv.at[d, o], sib if o else row, (col + d) % nc,
            )
    copies += list(x_copies.values()) + list(w_copies.values())

    y, x = positions()
    for h in range(2):
        xcol[h, DEPTH:PADDED, :] = jnp.zeros((PADDED - DEPTH, VOX), BF16)
    low_ok = (col > 0).astype(F32)
    high_ok = (col < nc - 1).astype(F32)
    for a in (1, 0, 2):
        for o in range(2):
            if (a, o) in x_copies:
                x_copies[a, o].wait_recv()
        for h in range(2):
            plane = xin[a, CH * h : CH * h + CH, :].astype(F32)
            if a == 0:
                plane = plane * low_ok
            if a == 2:
                plane = plane * high_ok
            for b in range(3):
                for c in range(3):
                    tap = 9 * a + 3 * b + c
                    xcol[h, CH * tap : CH * tap + CH, :] = moved_view(plane, y, x, b - 1, c - 1).astype(BF16)

    for copy in w_copies.values():
        copy.wait_recv()
    ypart[...] = (
        jnp.dot(wg[0], xcol[0], preferred_element_type=F32)
        + jnp.dot(wg[1], xcol[1], preferred_element_type=F32)
    ).astype(BF16)

    y_copies = []
    for j in range(1, nc):
        owner = (q + j) % nc
        y_copies.append(
            send(
                ypart.at[rows(CH * ((col - owner + nc) % nc)), :], yrecv.at[j],
                y_send.at[j], y_recv.at[j], 2 * owner + k, col,
            )
        )
    copies += y_copies
    slot = rows(CH * ((col - q + nc) % nc))
    sectioned = ypart[slot, :].astype(F32)
    tail = wg[0, slot, PADDED - 128 : PADDED].astype(F32)
    lane = lax.broadcasted_iota(jnp.int32, (CH, 128), 1)
    own_bias = jnp.sum(jnp.where(lane == DEPTH - (PADDED - 128), tail, 0.0), axis=1, keepdims=True)
    for j, copy in enumerate(y_copies):
        copy.wait_recv()
        sectioned = sectioned + yrecv[j + 1].astype(F32)
    sectioned = sectioned + own_bias
    s = 1.0 / (1.0 + jnp.exp(-sectioned))
    out_ref[...] = (sectioned * s).astype(BF16)
    g[slot, :] = (cot_ref[...].astype(F32) * (s * (1.0 + sectioned * (1.0 - s)))).astype(BF16)

    g_copies = []
    for j in range(1, nc):
        g_copies.append(
            send(
                g.at[slot, :], g.at[slot, :], g_send.at[j], g_recv.at[j], 2 * ((q + j) % nc) + k, col
            )
        )
    bias_part = lax.dot_general(
        jnp.ones((8, VOX), BF16), g[slot, :], (((1,), (1,)), ((), ())), preferred_element_type=F32
    )
    bsend[:, 0:CH] = bias_part
    b_copies = []
    for d in range(1, nc):
        b_copies.append(
            send(bsend, brecv.at[d], b_send.at[d], b_recv.at[d], row, (col + d) % nc)
        )
    copies += g_copies + b_copies

    for copy in g_copies:
        copy.wait_recv()
    for h in range(2):
        wgp[h] = lax.dot_general(
            g[...], xcol[h], (((1,), (1,)), ((), ())), preferred_element_type=F32
        ).astype(BF16)
    wg_copies = []
    for d in range(nc):
        for o in range(2):
            h = 1 - k if o else k
            if d == 0 and o == 0:
                wgrecv[0, rows(CH * k), :] = wgp[k, 0:CH, :]
                continue
            wg_copies.append(
                send(
                    wgp.at[h, pl.ds(CH * d, CH), :], wgrecv.at[d, rows(CH * k), :],
                    wg_send.at[d, o], wg_recv.at[d, o], sib if o else row, (col - d + nc) % nc,
                )
            )
    copies += wg_copies

    for h in range(2):
        z[...] = lax.dot_general(
            wg[h], g[...], (((0,), (0,)), ((), ())), preferred_element_type=F32
        )
        for a in range(3):
            total = jnp.zeros((CH, VOX), F32)
            for b in range(3):
                for c in range(3):
                    tap = 9 * a + 3 * b + c
                    total = total + moved_view(z[CH * tap : CH * tap + CH, :], y, x, 1 - b, 1 - c)
            dsend[a, CH * h : CH * h + CH, :] = total.astype(BF16)
            if a == 1:
                dacc[h] = total
    d_copies = []
    for o in range(2):
        mine = rows(CH * (1 - k if o else k))
        for a, to_col in ((1, col), (2, up), (0, down)):
            if a == 1 and o == 0:
                continue
            d_copies.append(
                send(
                    dsend.at[a, mine, :], drecv.at[a, o], d_send.at[a, o], d_recv.at[a, o],
                    sib if o else row, to_col,
                )
            )
    copies += d_copies

    for copy in b_copies:
        copy.wait_recv()
    bias_sum = bsend[...]
    for d in range(1, nc):
        bias_sum = bias_sum + brecv[d]
    bgrad_ref[...] = bias_sum[0:1, 0:CH] * norm_factor

    for copy in d_copies:
        copy.wait_recv()
    data_sum = dacc[k] + drecv[1, 1].astype(F32)
    data_sum = data_sum + low_ok * (drecv[2, 0].astype(F32) + drecv[2, 1].astype(F32))
    data_sum = data_sum + high_ok * (drecv[0, 0].astype(F32) + drecv[0, 1].astype(F32))
    dgrad_ref[...] = data_sum.astype(BF16)

    for copy in wg_copies:
        copy.wait_recv()
    total = wgrecv[0].astype(F32)
    for d in range(1, nc):
        total = total + wgrecv[d].astype(F32)
    total = jnp.transpose(total * norm_factor)
    wgrad_ref[...] = total[0:DEPTH].reshape(TAPS, CH, 2 * CH)

    for copy in copies:
        copy.wait_send()


def on_device(nc, volume, filters, bias, cotangent):
    chunk = CH * nc
    dma = pltpu.SemaphoreType.DMA
    vmem = pl.BlockSpec(memory_space=pltpu.VMEM)
    output, data_grad, weight_grad, bias_grad = pl.pallas_call(
        functools.partial(kernel, nc, 1.0 / math.sqrt(nc * VOX)),
        out_shape=(
            jax.ShapeDtypeStruct((CH, VOX), BF16),
            jax.ShapeDtypeStruct((CH, VOX), BF16),
            jax.ShapeDtypeStruct((TAPS, CH, 2 * CH), F32),
            jax.ShapeDtypeStruct((1, CH), F32),
        ),
        in_specs=[vmem] * 4,
        out_specs=(vmem,) * 4,
        scratch_shapes=[
            pltpu.VMEM((PADDED, 128), F32),
            pltpu.VMEM((2 * CH, PADDED), BF16),
            pltpu.VMEM((2, chunk, PADDED), BF16),
            pltpu.VMEM((3, 2 * CH, VOX), BF16),
            pltpu.VMEM((2, PADDED, VOX), BF16),
            pltpu.VMEM((chunk, VOX), BF16),
            pltpu.VMEM((nc, CH, VOX), BF16),
            pltpu.VMEM((chunk, VOX), BF16),
            pltpu.VMEM((2, chunk, PADDED), BF16),
            pltpu.VMEM((nc, 2 * CH, PADDED), BF16),
            pltpu.VMEM((8, 128), F32),
            pltpu.VMEM((nc, 8, 128), F32),
            pltpu.VMEM((PADDED, VOX), F32),
            pltpu.VMEM((3, 2 * CH, VOX), BF16),
            pltpu.VMEM((2, CH, VOX), F32),
            pltpu.VMEM((3, 2, CH, VOX), BF16),
            dma((3, 2)), dma((3, 2)),
            dma((nc, 2)), dma((nc, 2)),
            dma((nc,)), dma((nc,)),
            dma((nc,)), dma((nc,)),
            dma((nc,)), dma((nc,)),
            dma((nc, 2)), dma((nc, 2)),
            dma((3, 2)), dma((3, 2)),
        ],
        compiler_params=pltpu.CompilerParams(
            collective_id=0, has_side_effects=True, vmem_limit_bytes=48 * 1024 * 1024
        ),
    )(volume, filters, bias.reshape(1, 2 * CH), cotangent)
    return output, data_grad, weight_grad, bias_grad.reshape(CH)


def solution(mesh):
    placed = (P("row", "col"), P(None, "row", "col"), P("col"), P("row", "col"))
    return jax.shard_map(
        functools.partial(on_device, mesh.shape["col"]),
        mesh=mesh,
        in_specs=placed,
        out_specs=(P("row", "col"), P("row", "col"), P(None, "row", "col"), P("row")),
        check_vma=False,
    )
```

```python
import functools
import math

import jax
import jax.numpy as jnp
from jax import lax
from jax.experimental import pallas as pl
from jax.experimental.pallas import tpu as pltpu
from jax.sharding import PartitionSpec as P

S = 32
VOX = S * S
CH = 32
TAPS = 27
DEPTH = TAPS * CH
PADDED = 896
LAST = PADDED - 128
MESH = pl.DeviceIdType.MESH
BF16 = jnp.bfloat16
F32 = jnp.float32
VMEM_LIMIT = 56 * 1024 * 1024
NT = (((1,), (1,)), ((), ()))
TN = (((0,), (0,)), ((), ()))


def inside(coord, step):
    moved = coord + step
    return (moved >= 0) & (moved < S)


def moved_view(value, y, x, dy, dx):
    offset = dy * S + dx
    if offset:
        value = pltpu.roll(value, (-offset) % VOX, 1)
    if dy or dx:
        value = jnp.where(inside(y, dy) & inside(x, dx), value, 0.0)
    return value


def kernel(
    nc, norm_factor,
    vol_hbm, w_hbm, bias_hbm, cot_hbm,
    out_hbm, dgrad_hbm, wsum_hbm, bsum_hbm,
    w_own, bias_own, cot, wpad, wt_own, wg, xin, xcol, ypart, yrecv, g, wgp, wgz, wzsum, wgrecv, bsend, brecv,
    z, dsib, dsib_recv, dnear, dhalo, dhalo_recv, out_v, dgrad_v, wsum_v, bsum_v,
    load_sem, store_sem, x_send, x_recv, xs_send, xs_recv, w_send, w_recv, wf_send, wf_recv,
    y_send, y_recv, g_send, g_recv, b_send, b_recv, p_send, p_recv, pz_send, pz_recv, pf_send, pf_recv,
    d_send, d_recv, h_send, h_recv,
):
    row = lax.axis_index("row")
    col = lax.axis_index("col")
    q = row // 2
    k = row % 2
    sib = 2 * q + 1 - k
    ny = nc // 2
    ypos = col // 2
    zpos = col % 2
    pair = 2 * ypos + 1 - zpos
    up = (col + 1) % nc
    down = (col + nc - 1) % nc

    def rows(start, size=CH):
        return pl.ds(pl.multiple_of(start, CH), size)

    def y_col(step):
        return 2 * ((ypos + step + ny) % ny) + zpos

    def owner(dy, dz):
        zo = 1 - zpos if dz else zpos
        return 2 * ((ypos - dy + ny) % ny) + zo

    def remote(src, dst, send_sem, recv_sem, to_row, to_col):
        return pltpu.make_async_remote_copy(
            src_ref=src, dst_ref=dst, send_sem=send_sem, recv_sem=recv_sem,
            device_id=(to_row, to_col), device_id_type=MESH,
        )

    copies = []

    def send(*args):
        copy = remote(*args)
        copy.start()
        copies.append(copy)
        return copy

    load_w = pltpu.make_async_copy(w_hbm, w_own, load_sem.at[0])
    load_bias = pltpu.make_async_copy(bias_hbm, bias_own, load_sem.at[1])
    load_vol = pltpu.make_async_copy(vol_hbm, xin.at[1, rows(CH * k), :], load_sem.at[2])
    load_cot = pltpu.make_async_copy(cot_hbm, cot, load_sem.at[3])
    for load in (load_w, load_bias, load_vol, load_cot):
        load.start()

    barrier = pltpu.get_barrier_semaphore()
    peers = [(sib, col), (row, pair), (sib, pair)]
    peers += [(row, up), (row, down)]
    for dy in range(1, ny):
        peers += [(row, y_col(dy)), (sib, y_col(dy)), (row, 2 * ((ypos + dy) % ny) + 1 - zpos)]
    for j in range(1, nc):
        peers.append((2 * ((q + j) % nc) + k, col))
    for peer in peers:
        pl.semaphore_signal(barrier, inc=1, device_id=peer, device_id_type=MESH)

    wpad[...] = jnp.zeros_like(wpad)
    bsend[...] = jnp.zeros_like(bsend)
    load_w.wait()
    load_bias.wait()
    wpad[0:DEPTH, 0 : 2 * CH] = w_own[...].reshape(DEPTH, 2 * CH).astype(F32)
    wpad[DEPTH : DEPTH + 1, 0 : 2 * CH] = bias_own[...].astype(F32)
    wt_own[...] = jnp.transpose(wpad[...])[0 : 2 * CH].astype(BF16)
    load_vol.wait()
    mine, other = rows(CH * k), rows(CH * (1 - k))

    pl.semaphore_wait(barrier, len(peers))

    def slot(dy, dz):
        return CH * (dz * ny + dy)

    def slot_rows(dy, dz):
        return pl.ds(slot(dy, dz), CH)

    w_copies = {}

    def send_weights(dy, dz, to_col):
        for o in range(2):
            if (dy, dz, o) == (0, 0, 0):
                continue
            w_copies[dy, dz, o] = send(
                wt_own.at[other if o else mine, :], wg.at[k, slot_rows(dy, dz), :],
                w_send.at[dz * ny + dy, o], w_recv.at[dz * ny + dy, o], sib if o else row, to_col,
            )

    send_weights(0, 1, pair)
    x_sib = send(xin.at[1, mine, :], xin.at[1, mine, :], xs_send.at[1], xs_recv.at[1], sib, col)
    send_weights(0, 0, col)
    for dy in (1, 3, 2):
        if dy < ny:
            send_weights(dy, 0, y_col(dy))
    x_halo = {
        0: send(xin.at[1, mine, :], xin.at[0, mine, :], x_send.at[0], x_recv.at[0], row, up),
        2: send(xin.at[1, mine, :], xin.at[2, mine, :], x_send.at[2], x_recv.at[2], row, down),
    }
    wg[k, slot_rows(0, 0), :] = wt_own[mine, :]

    lane = lax.broadcasted_iota(jnp.int32, (CH, VOX), 1)
    y, x = lane // S, lane % S
    low_ok = (col > 0).astype(F32)
    high_ok = (col < nc - 1).astype(F32)
    for h in range(2):
        xcol[h, DEPTH:PADDED, :] = jnp.zeros((PADDED - DEPTH, VOX), BF16)

    def fill(a, h):
        plane = xin[a, rows(CH * h), :].astype(F32)
        if a == 0:
            plane = plane * low_ok
        if a == 2:
            plane = plane * high_ok
        for b in range(3):
            for c in range(3):
                tap = 9 * a + 3 * b + c
                xcol[h, CH * tap : CH * tap + CH, :] = moved_view(plane, y, x, b - 1, c - 1).astype(BF16)

    fill(1, k)
    for o in range(2):
        w_copies[0, 1, o].wait_recv()
    wf_copies = []
    for dy in (1, 3, 2):
        if dy < ny:
            wf_copies.append(
                send(
                    wg.at[:, slot_rows(0, 1), :], wg.at[:, slot_rows(dy, 1), :],
                    wf_send.at[dy], wf_recv.at[dy], row, y_col(dy),
                )
            )
    x_sib.wait_recv()
    fill(1, 1 - k)
    x_forward = {}
    for a in (0, 2):
        x_halo[a].wait_recv()
        x_forward[a] = send(xin.at[a, mine, :], xin.at[a, mine, :], xs_send.at[a], xs_recv.at[a], sib, col)
    for a in (0, 2):
        fill(a, k)
    for a in (0, 2):
        x_forward[a].wait_recv()
        fill(a, 1 - k)

    later = []
    for dz in range(2):
        if dz == 0:
            w_copies[0, 0, 1].wait_recv()
            for dy in range(1, ny):
                for o in range(2):
                    w_copies[dy, 0, o].wait_recv()
        else:
            for copy in wf_copies:
                copy.wait_recv()
        half = pl.ds(CH * ny * dz, CH * ny)
        ypart[half, :] = (
            jnp.dot(wg[0, half, :], xcol[0], preferred_element_type=F32)
            + jnp.dot(wg[1, half, :], xcol[1], preferred_element_type=F32)
        ).astype(BF16)
        for dy in range(ny):
            to = owner(dy, dz)
            copy = remote(
                ypart.at[slot_rows(dy, dz), :], yrecv.at[q],
                y_send.at[dz * ny + dy], y_recv.at[q], 2 * to + k, col,
            )

            @pl.when(to != q)
            def _():
                copy.start()

            later.append((to != q, copy))

    def from_pair(index, dst, sem):
        return remote(dst, dst, sem, sem, 2 * index + k, col)

    own_slot = rows(CH * ((q % 2 != zpos).astype(jnp.int32) * ny + (ypos - q // 2 + ny) % ny))
    sectioned = ypart[own_slot, :].astype(F32)
    tail = wg[0, own_slot, LAST:PADDED].astype(F32)
    tail_lane = lax.broadcasted_iota(jnp.int32, (CH, 128), 1)
    own_bias = jnp.sum(jnp.where(tail_lane == DEPTH - LAST, tail, 0.0), axis=1, keepdims=True)
    load_cot.wait()
    for j in range(1, nc):
        source = (q + j) % nc
        from_pair(source, yrecv.at[source], y_recv.at[source]).wait_recv()
    for j in range(1, nc):
        sectioned = sectioned + yrecv[(q + j) % nc].astype(F32)
    sectioned = sectioned + own_bias
    s = 1.0 / (1.0 + jnp.exp(-sectioned))
    g[own_slot, :] = (cot[...].astype(F32) * (s * (1.0 + sectioned * (1.0 - s)))).astype(BF16)
    for j in range(1, nc):
        send(g.at[own_slot, :], g.at[own_slot, :], g_send.at[j], g_recv.at[q], 2 * ((q + j) % nc) + k, col)
    out_v[...] = (sectioned * s).astype(BF16)
    store_out = pltpu.make_async_copy(out_v, out_hbm, store_sem.at[0])
    store_out.start()

    bsend[:, 0:CH] = lax.dot_general(jnp.ones((8, VOX), BF16), g[own_slot, :], NT, preferred_element_type=F32)
    b_copies = []
    for d in range(1, nc):
        b_copies.append(send(bsend, brecv.at[d], b_send.at[d], b_recv.at[d], row, (col + d) % nc))

    p_copies = []
    pf_copies = []
    for dz in (1, 0):
        for dy in range(ny):
            source = owner(dy, dz)

            @pl.when(source != q)
            def _():
                part = g.at[slot_rows(dy, dz), :]
                from_pair(source, part, g_recv.at[source]).wait_recv()

        half = pl.ds(CH * ny * dz, CH * ny)
        for h in range(2):
            wgp[h, half, :] = lax.dot_general(g[half, :], xcol[h], NT, preferred_element_type=F32).astype(BF16)
        for dy in (1, 3, 2, 0):
            if dy >= ny:
                continue
            if dz and dy:
                p_copies.append(
                    send(
                        wgp.at[:, slot_rows(dy, 1), :], wgz.at[dy],
                        p_send.at[dy], p_recv.at[dy], row, y_col(-dy),
                    )
                )
            elif not dz:
                for o in range(2):
                    if dy or o:
                        pf_copies.append(
                            send(
                                wgp.at[1 - k if o else k, slot_rows(dy, 0), :], wgrecv.at[dy, mine, :],
                                pf_send.at[dy, o], pf_recv.at[dy, o], sib if o else row, y_col(-dy),
                            )
                        )
    wgrecv[0, mine, :] = wgp[k, slot_rows(0, 0), :]

    def spread(h):
        z[...] = lax.dot_general(wg[h], g[...], TN, preferred_element_type=F32)
        planes = []
        for a in range(3):
            total = jnp.zeros((CH, VOX), F32)
            for b in range(3):
                for c in range(3):
                    tap = 9 * a + 3 * b + c
                    total = total + moved_view(z[CH * tap : CH * tap + CH, :], y, x, 1 - b, 1 - c)
            planes.append(total)
        return planes

    for a, total in enumerate(spread(1 - k)):
        dsib[a] = total.astype(BF16)
    d_copy = send(dsib, dsib_recv, d_send.at[0], d_recv.at[0], sib, col)

    for copy in p_copies:
        copy.wait_recv()
    for h in range(2):
        total = wgp[h, slot_rows(0, 1), :].astype(F32)
        for dy in range(1, ny):
            total = total + wgz[dy, h].astype(F32)
        wzsum[h] = total.astype(BF16)
    for o in range(2):
        pf_copies.append(
            send(
                wzsum.at[1 - k if o else k], wgrecv.at[ny, mine, :],
                pz_send.at[o], pz_recv.at[o], sib if o else row, pair,
            )
        )

    for a, total in enumerate(spread(k)):
        dnear[a] = total
    d_copy.wait_recv()
    h_copies = []
    for a, to_col in ((0, down), (2, up)):
        dhalo[a] = (dnear[a] + dsib_recv[a].astype(F32)).astype(BF16)
        h_copies.append(send(dhalo.at[a], dhalo_recv.at[a], h_send.at[a], h_recv.at[a], row, to_col))
    near = dnear[1] + dsib_recv[1].astype(F32)

    for copy in b_copies:
        copy.wait_recv()
    bias_sum = bsend[...]
    for d in range(1, nc):
        bias_sum = bias_sum + brecv[d]
    bsum_v[...] = bias_sum * norm_factor
    store_bias = pltpu.make_async_copy(bsum_v, bsum_hbm, store_sem.at[3])
    store_bias.start()

    for copy in h_copies:
        copy.wait_recv()
    near = near + low_ok * dhalo_recv[2].astype(F32) + high_ok * dhalo_recv[0].astype(F32)
    dgrad_v[...] = near.astype(BF16)
    store_data = pltpu.make_async_copy(dgrad_v, dgrad_hbm, store_sem.at[1])
    store_data.start()

    for copy in pf_copies:
        copy.wait_recv()
    total = wgrecv[0].astype(F32)
    for d in range(1, ny + 1):
        total = total + wgrecv[d].astype(F32)
    wsum_v[...] = total * norm_factor
    store_weights = pltpu.make_async_copy(wsum_v, wsum_hbm, store_sem.at[2])
    store_weights.start()

    for copy in copies:
        copy.wait_send()
    for sent, copy in later:

        @pl.when(sent)
        def _():
            copy.wait_send()

    for store in (store_out, store_data, store_weights, store_bias):
        store.wait()


def finish(
    out_in, dgrad_in, wsum_in, bsum_in, out_hbm, dgrad_hbm, wgrad_hbm, bgrad_hbm,
    out_v, dgrad_v, wsum_v, bsum_v, wgrad_v, bgrad_v, load_sem, store_sem,
):
    loads = [
        pltpu.make_async_copy(src, dst, load_sem.at[i])
        for i, (src, dst) in enumerate(
            ((wsum_in, wsum_v), (out_in, out_v), (dgrad_in, dgrad_v), (bsum_in, bsum_v))
        )
    ]
    stores = [
        pltpu.make_async_copy(src, dst, store_sem.at[i])
        for i, (src, dst) in enumerate(
            ((wgrad_v, wgrad_hbm), (out_v, out_hbm), (dgrad_v, dgrad_hbm), (bgrad_v, bgrad_hbm))
        )
    ]
    for load in loads:
        load.start()
    for i in (1, 2):
        loads[i].wait()
        stores[i].start()
    loads[3].wait()
    bgrad_v[...] = bsum_v[0:1, 0:CH]
    stores[3].start()
    loads[0].wait()
    wgrad_v[...] = jnp.transpose(wsum_v[...])[0:DEPTH].reshape(TAPS, CH, 2 * CH)
    stores[0].start()
    for store in stores:
        store.wait()


def on_device(nc, volume, filters, bias, cotangent):
    ny = nc // 2
    chunk = CH * nc
    dma = pltpu.SemaphoreType.DMA
    hbm = pl.BlockSpec(memory_space=pl.ANY)
    plane = (CH, VOX)
    sums = pl.pallas_call(
        functools.partial(kernel, nc, 1.0 / math.sqrt(nc * VOX)),
        out_shape=(
            jax.ShapeDtypeStruct(plane, BF16),
            jax.ShapeDtypeStruct(plane, BF16),
            jax.ShapeDtypeStruct((2 * CH, PADDED), F32),
            jax.ShapeDtypeStruct((8, 128), F32),
        ),
        in_specs=[hbm] * 4,
        out_specs=(hbm,) * 4,
        scratch_shapes=[
            pltpu.VMEM((TAPS, CH, 2 * CH), BF16),
            pltpu.VMEM((1, 2 * CH), BF16),
            pltpu.VMEM(plane, BF16),
            pltpu.VMEM((PADDED, 128), F32),
            pltpu.VMEM((2 * CH, PADDED), BF16),
            pltpu.VMEM((2, chunk, PADDED), BF16),
            pltpu.VMEM((3, 2 * CH, VOX), BF16),
            pltpu.VMEM((2, PADDED, VOX), BF16),
            pltpu.VMEM((chunk, VOX), BF16),
            pltpu.VMEM((nc, CH, VOX), BF16),
            pltpu.VMEM((chunk, VOX), BF16),
            pltpu.VMEM((2, chunk, PADDED), BF16),
            pltpu.VMEM((ny, 2, CH, PADDED), BF16),
            pltpu.VMEM((2, CH, PADDED), BF16),
            pltpu.VMEM((ny + 1, 2 * CH, PADDED), BF16),
            pltpu.VMEM((8, 128), F32),
            pltpu.VMEM((nc, 8, 128), F32),
            pltpu.VMEM((PADDED, VOX), F32),
            pltpu.VMEM((3, CH, VOX), BF16),
            pltpu.VMEM((3, CH, VOX), BF16),
            pltpu.VMEM((3, CH, VOX), F32),
            pltpu.VMEM((3, CH, VOX), BF16),
            pltpu.VMEM((3, CH, VOX), BF16),
            pltpu.VMEM(plane, BF16),
            pltpu.VMEM(plane, BF16),
            pltpu.VMEM((2 * CH, PADDED), F32),
            pltpu.VMEM((8, 128), F32),
            dma((4,)), dma((4,)),
            dma((3,)), dma((3,)), dma((3,)), dma((3,)),
            dma((nc, 2)), dma((nc, 2)), dma((ny,)), dma((ny,)),
            dma((nc,)), dma((nc,)), dma((nc,)), dma((nc,)), dma((nc,)), dma((nc,)),
            dma((ny,)), dma((ny,)), dma((2,)), dma((2,)), dma((ny, 2)), dma((ny, 2)),
            dma((1,)), dma((1,)), dma((3,)), dma((3,)),
        ],
        compiler_params=pltpu.CompilerParams(
            collective_id=0, has_side_effects=True, vmem_limit_bytes=VMEM_LIMIT
        ),
    )(volume, filters, bias.reshape(1, 2 * CH), cotangent)
    output, data_grad, weight_grad, bias_grad = pl.pallas_call(
        finish,
        out_shape=(
            jax.ShapeDtypeStruct(plane, BF16),
            jax.ShapeDtypeStruct(plane, BF16),
            jax.ShapeDtypeStruct((TAPS, CH, 2 * CH), F32),
            jax.ShapeDtypeStruct((1, CH), F32),
        ),
        in_specs=[hbm] * 4,
        out_specs=(hbm,) * 4,
        scratch_shapes=[
            pltpu.VMEM(plane, BF16),
            pltpu.VMEM(plane, BF16),
            pltpu.VMEM((2 * CH, PADDED), F32),
            pltpu.VMEM((8, 128), F32),
            pltpu.VMEM((TAPS, CH, 2 * CH), F32),
            pltpu.VMEM((1, CH), F32),
            dma((4,)), dma((4,)),
        ],
        compiler_params=pltpu.CompilerParams(vmem_limit_bytes=VMEM_LIMIT),
    )(*sums)
    return output, data_grad, weight_grad, bias_grad.reshape(CH)


def solution(mesh):
    placed = (P("row", "col"), P(None, "row", "col"), P("col"), P("row", "col"))
    return jax.shard_map(
        functools.partial(on_device, mesh.shape["col"]),
        mesh=mesh,
        in_specs=placed,
        out_specs=(P("row", "col"), P("row", "col"), P(None, "row", "col"), P("row")),
        check_vma=False,
    )
```

```python
import functools
import math

import jax
import jax.numpy as jnp
from jax import lax
from jax.experimental import pallas as pl
from jax.experimental.pallas import tpu as pltpu
from jax.sharding import PartitionSpec as P

S = 32
VOX = S * S
CH = 32
TAPS = 27
DEPTH = TAPS * CH
HALF = CH // 2
VIEWS = 9 * CH
PADDED = 896
LAST = PADDED - 128
MESH = pl.DeviceIdType.MESH
BF16 = jnp.bfloat16
F32 = jnp.float32
VMEM_LIMIT = 56 * 1024 * 1024
NT = (((1,), (1,)), ((), ()))
TN = (((0,), (0,)), ((), ()))


def inside(coord, step):
    moved = coord + step
    return (moved >= 0) & (moved < S)


def moved_view(value, y, x, dy, dx):
    offset = dy * S + dx
    if offset:
        value = pltpu.roll(value, (-offset) % VOX, 1)
    if dy or dx:
        value = jnp.where(inside(y, dy) & inside(x, dx), value, 0.0)
    return value


def kernel(
    nc, norm_factor,
    vol_hbm, w_hbm, bias_hbm, cot_hbm,
    out_hbm, dgrad_hbm, wsum_hbm, bsum_hbm,
    w_own, bias_own, cot, wpad, wt_own, wg, xin, xcol, ypart, yrecv, gown, g, wgp, wgrecv, bsend, brecv,
    z, dsib, dsib_recv, dnear, dfar, dfar_recv, out_v, dgrad_v, wsum_v, bsum_v,
    load_sem, store_sem, x_send, x_recv, xs_send, xs_recv, w_send, w_recv,
    y_send, y_recv, g_send, g_recv, b_send, b_recv, p_send, p_recv, d_send, d_recv, h_send, h_recv,
):
    row = lax.axis_index("row")
    col = lax.axis_index("col")
    q = row // 2
    k = row % 2
    sib = 2 * q + 1 - k
    ny = nc // 2
    xpos = q // 2
    zlow = q % 2
    ypos = col // 2
    zpos = col % 2
    pair = 2 * ypos + 1 - zpos

    def rows(start, size=CH):
        return pl.ds(pl.multiple_of(start, CH), size)

    def around(position):
        return (position + 2 * ny) % ny

    def half_rows(start):
        return pl.ds(pl.multiple_of(start, HALF), HALF)

    def flip(position, other_one):
        return 1 - position if other_one else position

    steps = [dx for dx in (1, 3, 2, 0) if dx < ny]
    col_steps = [(dy, dz) for dy in steps for dz in (1, 0)]
    row_steps = [(dx, a, p) for dx in steps for a in (1, 0) for p in (1, 0)]

    def col_at(dy, dz):
        return 2 * around(ypos + dy) + flip(zpos, dz)

    def pair_at(dx, a):
        return 2 * around(xpos + dx) + flip(zlow, a)

    def remote(src, dst, send_sem, recv_sem, to_row, to_col):
        return pltpu.make_async_remote_copy(
            src_ref=src, dst_ref=dst, send_sem=send_sem, recv_sem=recv_sem,
            device_id=(to_row, to_col), device_id_type=MESH,
        )

    copies = []

    def send(*args):
        copy = remote(*args)
        copy.start()
        copies.append(copy)
        return copy

    def arrived(dst, sem):
        remote(dst, dst, sem, sem, sib, col).wait_recv()

    load_w = pltpu.make_async_copy(w_hbm, w_own, load_sem.at[0])
    load_bias = pltpu.make_async_copy(bias_hbm, bias_own, load_sem.at[1])
    mine, other = rows(CH * k), rows(CH * (1 - k))
    load_vol = pltpu.make_async_copy(vol_hbm, xin.at[1 + zpos, mine, :], load_sem.at[2])
    load_cot = pltpu.make_async_copy(cot_hbm, cot, load_sem.at[3])
    for load in (load_w, load_bias, load_vol, load_cot):
        load.start()

    barrier = pltpu.get_barrier_semaphore()
    peers = [(sib if o else row, col_at(dy, dz)) for dy, dz in col_steps for o in range(2) if dy or dz or o]
    peers += [(2 * pair_at(dx, a) + k, 2 * ypos + flip(zpos, p)) for dx, a, p in row_steps if dx or a or p]
    for peer in peers:
        pl.semaphore_signal(barrier, inc=1, device_id=peer, device_id_type=MESH)

    wpad[...] = jnp.zeros_like(wpad)
    bsend[...] = jnp.zeros_like(bsend)
    wgp[:, :, LAST:PADDED] = jnp.zeros((2, HALF * nc, 128), BF16)
    load_w.wait()
    load_bias.wait()
    wpad[0:DEPTH, 0 : 2 * CH] = w_own[...].reshape(DEPTH, 2 * CH).astype(F32)
    wpad[DEPTH : DEPTH + 1, 0 : 2 * CH] = bias_own[...].astype(F32)
    wt_own[...] = jnp.transpose(wpad[...])[0 : 2 * CH].astype(BF16)
    load_vol.wait()

    pl.semaphore_wait(barrier, len(peers))

    own_plane = xin.at[1 + zpos, mine, :]
    x_sib = send(own_plane, own_plane, xs_send.at[0], xs_recv.at[0], sib, col)
    x_pair = send(own_plane, own_plane, x_send.at[0], x_recv.at[0], row, pair)
    side = around(ypos + 2 * zpos - 1)
    edge = xin.at[3 - 3 * zpos, mine, :]
    for i in range(2):
        send(own_plane, edge, x_send.at[1 + i], x_recv.at[2 - zpos], row, 2 * side + (zpos + i) % 2)

    own_rows = half_rows(HALF * col)
    w_copies = []
    for dy, dz in col_steps:
        for o in range(2):
            if dy or dz or o:
                part = half_rows(CH * flip(k, o) + HALF * flip(zpos, dz))
                w_copies.append(
                    send(
                        wt_own.at[part, :], wg.at[k, own_rows, :],
                        w_send.at[dy, dz, o], w_recv.at[dy, dz, o], sib if o else row, col_at(dy, dz),
                    )
                )
    wg[k, own_rows, :] = wt_own[half_rows(CH * k + HALF * zpos), :]

    lane = lax.broadcasted_iota(jnp.int32, (CH, VOX), 1)
    y, x = lane // S, lane % S
    low_ok = (ypos > 0).astype(F32)
    high_ok = (ypos < ny - 1).astype(F32)

    def fill(m, h, ok=None):
        plane = xin[m, rows(CH * h), :].astype(F32)
        if ok is not None:
            plane = plane * ok
        for b in range(3):
            for c in range(3):
                start = VIEWS * m + CH * (3 * b + c)
                xcol[h, rows(start), :] = moved_view(plane, y, x, b - 1, c - 1).astype(BF16)

    fill(1 + zpos, k)
    x_sib.wait_recv()
    fill(1 + zpos, 1 - k)
    to_sib = []
    x_pair.wait_recv()
    part = xin.at[2 - zpos, mine, :]
    to_sib.append(send(part, part, xs_send.at[1], xs_recv.at[1], sib, col))
    for i, m in ((1, 0), (2, 3)):
        part = xin.at[m, mine, :]
        arrived(part, x_recv.at[i])
        to_sib.append(send(part, part, xs_send.at[1 + i], xs_recv.at[1 + i], sib, col))
    fill(2 - zpos, k)
    fill(0, k, low_ok)
    fill(3, k, high_ok)
    for copy, m, ok in zip(to_sib, (2 - zpos, 0, 3), (None, low_ok, high_ok)):
        copy.wait_recv()
        fill(m, 1 - k, ok)

    chunk = HALF * nc
    for copy in w_copies:
        copy.wait_recv()
    tail = wg[0, :, LAST:PADDED].astype(F32)
    tail_lane = lax.broadcasted_iota(jnp.int32, (chunk, 128), 1)
    tail_row = lax.broadcasted_iota(jnp.int32, (chunk, 128), 0)
    with_bias = (tail_lane == DEPTH - LAST) & (tail_row // HALF == q)
    chunk_bias = jnp.sum(jnp.where(with_bias, tail, 0.0), axis=1, keepdims=True)
    for p in range(2):
        taps = pl.ds(VIEWS * p, DEPTH)
        ypart[p] = (
            jnp.dot(wg[0, :, 0:DEPTH], xcol[0, taps, :], preferred_element_type=F32)
            + jnp.dot(wg[1, :, 0:DEPTH], xcol[1, taps, :], preferred_element_type=F32)
            + chunk_bias
        ).astype(BF16)
    y_copies = []
    for dx, a, p in row_steps:
        to = pair_at(dx, a)
        plane = flip(zpos, p)
        part = half_rows(HALF * to)
        if dx or a or p:
            y_copies.append(
                send(
                    ypart.at[plane, part, :], yrecv.at[2 * dx + a, half_rows(HALF * zpos), :],
                    y_send.at[2 * dx + a, p], y_recv.at[2 * dx + a, p], 2 * to + k, 2 * ypos + plane,
                )
            )
        else:
            yrecv[0, half_rows(HALF * zpos), :] = ypart[plane, part, :]

    load_cot.wait()
    for copy in y_copies:
        copy.wait_recv()
    sectioned = yrecv[0].astype(F32)
    for j in range(1, nc):
        sectioned = sectioned + yrecv[j].astype(F32)
    s = 1.0 / (1.0 + jnp.exp(-sectioned))
    gown[...] = (cot[...].astype(F32) * (s * (1.0 + sectioned * (1.0 - s)))).astype(BF16)
    g_copies = []
    own_rows = half_rows(HALF * q)
    for dx, a, p in row_steps:
        part = half_rows(HALF * flip(zpos, p))
        if dx or a or p:
            g_copies.append(
                send(
                    gown.at[part, :], g.at[zpos, own_rows, :], g_send.at[2 * dx + a, p], g_recv.at[2 * dx + a, p],
                    2 * pair_at(dx, a) + k, 2 * ypos + flip(zpos, p),
                )
            )
        else:
            g[zpos, own_rows, :] = gown[part, :]

    out_v[...] = (sectioned * s).astype(BF16)
    store_out = pltpu.make_async_copy(out_v, out_hbm, store_sem.at[0])
    store_out.start()
    bsend[:, 0:CH] = lax.dot_general(jnp.ones((8, VOX), BF16), gown[...], NT, preferred_element_type=F32)
    b_copies = []
    for d in range(1, nc):
        b_copies.append(send(bsend, brecv.at[d], b_send.at[d], b_recv.at[d], row, (col + d) % nc))

    for copy in g_copies:
        copy.wait_recv()
    for h in range(2):
        total = jnp.zeros((chunk, DEPTH), F32)
        for p in range(2):
            total = total + lax.dot_general(
                g[p], xcol[h, VIEWS * p : VIEWS * p + DEPTH, :], NT, preferred_element_type=F32
            )
        wgp[h, :, 0:DEPTH] = total.astype(BF16)
    p_copies = []
    place = half_rows(CH * k + HALF * zpos)
    for dy, dz in col_steps:
        to = col_at(dy, dz)
        part = half_rows(HALF * to)
        for o in range(2):
            if dy or dz or o:
                p_copies.append(
                    send(
                        wgp.at[flip(k, o), part, :], wgrecv.at[dy, place, :],
                        p_send.at[dy, dz, o], p_recv.at[dy, dz, o], sib if o else row, to,
                    )
                )
            else:
                wgrecv[0, place, :] = wgp[k, part, :]

    def spread(h):
        for p in range(2):
            z[p] = lax.dot_general(wg[h], g[p], TN, preferred_element_type=F32)
        planes = []
        for m in range(4):
            total = jnp.zeros((CH, VOX), F32)
            for b in range(3):
                for c in range(3):
                    part = None
                    for p in range(2):
                        if 0 <= m - p <= 2:
                            start = VIEWS * (m - p) + CH * (3 * b + c)
                            term = z[p, start : start + CH, :]
                            part = term if part is None else part + term
                    total = total + moved_view(part, y, x, 1 - b, 1 - c)
            planes.append(total)
        return planes

    for m, total in enumerate(spread(1 - k)):
        dsib[m] = total.astype(BF16)
    d_copy = send(dsib, dsib_recv, d_send.at[0], d_recv.at[0], sib, col)
    for m, total in enumerate(spread(k)):
        dnear[m] = total
    d_copy.wait_recv()
    for m in range(4):
        dnear[m] = dnear[m] + dsib_recv[m].astype(F32)
    dfar[0] = dnear[0].astype(BF16)
    dfar[1] = dnear[2 - zpos].astype(BF16)
    dfar[2] = dnear[3].astype(BF16)
    send(dfar.at[0], dfar_recv.at[1 + zpos], h_send.at[0], h_recv.at[1 + zpos], row, 2 * around(ypos - 1) + 1)
    send(dfar.at[1], dfar_recv.at[0], h_send.at[1], h_recv.at[0], row, pair)
    send(dfar.at[2], dfar_recv.at[1 + zpos], h_send.at[2], h_recv.at[1 + zpos], row, 2 * around(ypos + 1))

    for copy in b_copies:
        copy.wait_recv()
    bias_sum = bsend[...]
    for d in range(1, nc):
        bias_sum = bias_sum + brecv[d]
    bsum_v[...] = bias_sum * norm_factor
    store_bias = pltpu.make_async_copy(bsum_v, bsum_hbm, store_sem.at[3])
    store_bias.start()

    for i in range(3):
        arrived(dfar_recv.at[i], h_recv.at[i])
    edge_ok = jnp.where(zpos == 1, high_ok, low_ok)
    near_sum = dnear[1 + zpos] + dfar_recv[0].astype(F32)
    near_sum = near_sum + edge_ok * (dfar_recv[1].astype(F32) + dfar_recv[2].astype(F32))
    dgrad_v[...] = near_sum.astype(BF16)
    store_data = pltpu.make_async_copy(dgrad_v, dgrad_hbm, store_sem.at[1])
    store_data.start()

    for copy in p_copies:
        copy.wait_recv()
    total = wgrecv[0].astype(F32)
    for d in range(1, ny):
        total = total + wgrecv[d].astype(F32)
    wsum_v[...] = total * norm_factor
    store_weights = pltpu.make_async_copy(wsum_v, wsum_hbm, store_sem.at[2])
    store_weights.start()

    for copy in copies:
        copy.wait_send()
    for store in (store_out, store_data, store_weights, store_bias):
        store.wait()


def finish(
    out_in, dgrad_in, wsum_in, bsum_in, out_hbm, dgrad_hbm, wgrad_hbm, bgrad_hbm,
    out_v, dgrad_v, wsum_v, bsum_v, wgrad_v, bgrad_v, load_sem, store_sem,
):
    loads = [
        pltpu.make_async_copy(src, dst, load_sem.at[i])
        for i, (src, dst) in enumerate(
            ((wsum_in, wsum_v), (out_in, out_v), (dgrad_in, dgrad_v), (bsum_in, bsum_v))
        )
    ]
    stores = [
        pltpu.make_async_copy(src, dst, store_sem.at[i])
        for i, (src, dst) in enumerate(
            ((wgrad_v, wgrad_hbm), (out_v, out_hbm), (dgrad_v, dgrad_hbm), (bgrad_v, bgrad_hbm))
        )
    ]
    for load in loads:
        load.start()
    for i in (1, 2):
        loads[i].wait()
        stores[i].start()
    loads[3].wait()
    bgrad_v[...] = bsum_v[0:1, 0:CH]
    stores[3].start()
    loads[0].wait()
    wgrad_v[...] = jnp.transpose(wsum_v[...])[0:DEPTH].reshape(TAPS, CH, 2 * CH)
    stores[0].start()
    for store in stores:
        store.wait()


def on_device(nc, volume, filters, bias, cotangent):
    ny = nc // 2
    chunk = HALF * nc
    dma = pltpu.SemaphoreType.DMA
    hbm = pl.BlockSpec(memory_space=pl.ANY)
    plane = (CH, VOX)
    sums = pl.pallas_call(
        functools.partial(kernel, nc, 1.0 / math.sqrt(nc * VOX)),
        out_shape=(
            jax.ShapeDtypeStruct(plane, BF16),
            jax.ShapeDtypeStruct(plane, BF16),
            jax.ShapeDtypeStruct((2 * CH, PADDED), F32),
            jax.ShapeDtypeStruct((8, 128), F32),
        ),
        in_specs=[hbm] * 4,
        out_specs=(hbm,) * 4,
        scratch_shapes=[
            pltpu.VMEM((TAPS, CH, 2 * CH), BF16),
            pltpu.VMEM((1, 2 * CH), BF16),
            pltpu.VMEM(plane, BF16),
            pltpu.VMEM((PADDED, 128), F32),
            pltpu.VMEM((2 * CH, PADDED), BF16),
            pltpu.VMEM((2, chunk, PADDED), BF16),
            pltpu.VMEM((4, 2 * CH, VOX), BF16),
            pltpu.VMEM((2, 4 * VIEWS, VOX), BF16),
            pltpu.VMEM((2, chunk, VOX), BF16),
            pltpu.VMEM((nc, CH, VOX), BF16),
            pltpu.VMEM(plane, BF16),
            pltpu.VMEM((2, chunk, VOX), BF16),
            pltpu.VMEM((2, chunk, PADDED), BF16),
            pltpu.VMEM((ny, 2 * CH, PADDED), BF16),
            pltpu.VMEM((8, 128), F32),
            pltpu.VMEM((nc, 8, 128), F32),
            pltpu.VMEM((2, PADDED, VOX), F32),
            pltpu.VMEM((4, CH, VOX), BF16),
            pltpu.VMEM((4, CH, VOX), BF16),
            pltpu.VMEM((4, CH, VOX), F32),
            pltpu.VMEM((3, CH, VOX), BF16),
            pltpu.VMEM((3, CH, VOX), BF16),
            pltpu.VMEM(plane, BF16),
            pltpu.VMEM(plane, BF16),
            pltpu.VMEM((2 * CH, PADDED), F32),
            pltpu.VMEM((8, 128), F32),
            dma((4,)), dma((4,)),
            dma((3,)), dma((3,)), dma((4,)), dma((4,)),
            dma((ny, 2, 2)), dma((ny, 2, 2)),
            dma((nc, 2)), dma((nc, 2)), dma((nc, 2)), dma((nc, 2)), dma((nc,)), dma((nc,)),
            dma((ny, 2, 2)), dma((ny, 2, 2)), dma((1,)), dma((1,)), dma((3,)), dma((3,)),
        ],
        compiler_params=pltpu.CompilerParams(
            collective_id=0, has_side_effects=True, vmem_limit_bytes=VMEM_LIMIT
        ),
    )(volume, filters, bias.reshape(1, 2 * CH), cotangent)
    output, data_grad, weight_grad, bias_grad = pl.pallas_call(
        finish,
        out_shape=(
            jax.ShapeDtypeStruct(plane, BF16),
            jax.ShapeDtypeStruct(plane, BF16),
            jax.ShapeDtypeStruct((TAPS, CH, 2 * CH), F32),
            jax.ShapeDtypeStruct((1, CH), F32),
        ),
        in_specs=[hbm] * 4,
        out_specs=(hbm,) * 4,
        scratch_shapes=[
            pltpu.VMEM(plane, BF16),
            pltpu.VMEM(plane, BF16),
            pltpu.VMEM((2 * CH, PADDED), F32),
            pltpu.VMEM((8, 128), F32),
            pltpu.VMEM((TAPS, CH, 2 * CH), F32),
            pltpu.VMEM((1, CH), F32),
            dma((4,)), dma((4,)),
        ],
        compiler_params=pltpu.CompilerParams(vmem_limit_bytes=VMEM_LIMIT),
    )(*sums)
    return output, data_grad, weight_grad, bias_grad.reshape(CH)


def solution(mesh):
    placed = (P("row", "col"), P(None, "row", "col"), P("col"), P("row", "col"))
    return jax.shard_map(
        functools.partial(on_device, mesh.shape["col"]),
        mesh=mesh,
        in_specs=placed,
        out_specs=(P("row", "col"), P("row", "col"), P(None, "row", "col"), P("row")),
        check_vma=False,
    )
```

```python
import functools
import math

import jax
import jax.numpy as jnp
from jax import lax
from jax.experimental import pallas as pl
from jax.experimental.pallas import tpu as pltpu
from jax.sharding import PartitionSpec as P

S = 32
VOX = S * S
CH = 32
TAPS = 27
DEPTH = TAPS * CH
HALF = CH // 2
VIEWS = 9 * CH
PADDED = 896
LAST = PADDED - 128
MESH = pl.DeviceIdType.MESH
BF16 = jnp.bfloat16
F32 = jnp.float32
VMEM_LIMIT = 56 * 1024 * 1024
NT = (((1,), (1,)), ((), ()))
TN = (((0,), (0,)), ((), ()))


def inside(coord, step):
    moved = coord + step
    return (moved >= 0) & (moved < S)


def moved_view(value, y, x, dy, dx):
    offset = dy * S + dx
    if offset:
        value = pltpu.roll(value, (-offset) % VOX, 1)
    if dy or dx:
        value = jnp.where(inside(y, dy) & inside(x, dx), value, 0.0)
    return value


def kernel(
    nc, norm_factor,
    vol_hbm, w_hbm, bias_hbm, cot_hbm,
    out_hbm, dgrad_hbm, wsum_hbm, bsum_hbm,
    w_own, bias_own, cot, wpad, wt_own, wg, xin, xcol, ypart, yrecv, gown, g, wgp, wgrecv, bsend, brecv,
    z, dsib, dsib_recv, dnear, dfar, dfar_recv, out_v, dgrad_v, wsum_v, bsum_v,
    load_sem, store_sem, x_send, x_recv, xs_send, xs_recv, w_send, w_recv,
    y_send, y_recv, g_send, g_recv, b_send, b_recv, p_send, p_recv, d_send, d_recv, h_send, h_recv,
):
    row = lax.axis_index("row")
    col = lax.axis_index("col")
    q = row // 2
    k = row % 2
    sib = 2 * q + 1 - k
    ny = nc // 2
    xpos = q // 2
    zlow = q % 2
    ypos = col // 2
    zpos = col % 2
    pair = 2 * ypos + 1 - zpos

    def rows(start, size=CH):
        return pl.ds(pl.multiple_of(start, CH), size)

    def around(position):
        return (position + 2 * ny) % ny

    def half_rows(start):
        return pl.ds(pl.multiple_of(start, HALF), HALF)

    def flip(position, other_one):
        return 1 - position if other_one else position

    steps = [dx for dx in (1, 3, 2, 0) if dx < ny]
    col_steps = [(dy, dz) for dy in steps for dz in (1, 0)]
    row_steps = [(dx, a, p) for dx in steps for a in (1, 0) for p in (1, 0)]

    def col_at(dy, dz):
        return 2 * around(ypos + dy) + flip(zpos, dz)

    def pair_at(dx, a):
        return 2 * around(xpos + dx) + flip(zlow, a)

    def place(along, half):
        return half_rows(HALF * (ny * half + along))

    def remote(src, dst, send_sem, recv_sem, to_row, to_col):
        return pltpu.make_async_remote_copy(
            src_ref=src, dst_ref=dst, send_sem=send_sem, recv_sem=recv_sem,
            device_id=(to_row, to_col), device_id_type=MESH,
        )

    copies = []

    def send(*args):
        copy = remote(*args)
        copy.start()
        copies.append(copy)
        return copy

    def arrived(dst, sem):
        remote(dst, dst, sem, sem, sib, col).wait_recv()

    load_w = pltpu.make_async_copy(w_hbm, w_own, load_sem.at[0])
    load_bias = pltpu.make_async_copy(bias_hbm, bias_own, load_sem.at[1])
    mine, other = rows(CH * k), rows(CH * (1 - k))
    load_vol = pltpu.make_async_copy(vol_hbm, xin.at[1 + zpos, mine, :], load_sem.at[2])
    load_cot = pltpu.make_async_copy(cot_hbm, cot, load_sem.at[3])
    for load in (load_w, load_bias, load_vol, load_cot):
        load.start()

    barrier = pltpu.get_barrier_semaphore()
    peers = [(sib if o else row, col_at(dy, dz)) for dy, dz in col_steps for o in range(2) if dy or dz or o]
    peers += [(2 * pair_at(dx, a) + k, 2 * ypos + flip(zpos, p)) for dx, a, p in row_steps if dx or a or p]
    for peer in peers:
        pl.semaphore_signal(barrier, inc=1, device_id=peer, device_id_type=MESH)

    wpad[...] = jnp.zeros_like(wpad)
    bsend[...] = jnp.zeros_like(bsend)
    wgp[:, :, LAST:PADDED] = jnp.zeros((2, HALF * nc, 128), BF16)
    load_vol.wait()

    pl.semaphore_wait(barrier, len(peers))

    own_plane = xin.at[1 + zpos, mine, :]
    side = 2 * around(ypos + 2 * zpos - 1)
    edge = xin.at[3 - 3 * zpos, mine, :]
    for i in range(2):
        send(own_plane, edge, x_send.at[1 + i], x_recv.at[2 - zpos], row, side + flip(zpos, 1 - i))
    x_sib = send(own_plane, own_plane, xs_send.at[0], xs_recv.at[0], sib, col)
    x_pair = send(own_plane, own_plane, x_send.at[0], x_recv.at[0], row, pair)

    load_w.wait()
    load_bias.wait()
    wpad[0:DEPTH, 0 : 2 * CH] = w_own[...].reshape(DEPTH, 2 * CH).astype(F32)
    wpad[DEPTH : DEPTH + 1, 0 : 2 * CH] = bias_own[...].astype(F32)
    wt_own[...] = jnp.transpose(wpad[...])[0 : 2 * CH].astype(BF16)

    w_near, w_far = [], []
    for dz in range(2):
        for dy in (*steps[-1:], *steps[:-1]):
            for o in (1, 0):
                if dy or dz or o:
                    part = half_rows(CH * flip(k, o) + HALF * flip(zpos, dz))
                    (w_far if dz else w_near).append(
                        send(
                            wt_own.at[part, :], wg.at[k, place(ypos, dz), :],
                            w_send.at[dy, dz, o], w_recv.at[dy, dz, o], sib if o else row, col_at(dy, dz),
                        )
                    )
    wg[k, place(ypos, 0), :] = wt_own[half_rows(CH * k + HALF * zpos), :]

    lane = lax.broadcasted_iota(jnp.int32, (CH, VOX), 1)
    y, x = lane // S, lane % S
    low_ok = (ypos > 0).astype(F32)
    high_ok = (ypos < ny - 1).astype(F32)

    def fill(m, h, ok=None):
        plane = xin[m, rows(CH * h), :].astype(F32)
        if ok is not None:
            plane = plane * ok
        for b in range(3):
            for c in range(3):
                start = VIEWS * m + CH * (3 * b + c)
                xcol[h, rows(start), :] = moved_view(plane, y, x, b - 1, c - 1).astype(BF16)

    fill(1 + zpos, k)
    x_sib.wait_recv()
    fill(1 + zpos, 1 - k)
    to_sib = []
    for i, m in ((0, 2 - zpos), (1, 0), (2, 3)):
        part = xin.at[m, mine, :]
        arrived(part, x_recv.at[i])
        to_sib.append(send(part, part, xs_send.at[1 + i], xs_recv.at[1 + i], sib, col))
    fill(2 - zpos, k)
    fill(0, k, low_ok)
    fill(3, k, high_ok)
    for copy, m, ok in zip(to_sib, (2 - zpos, 0, 3), (None, low_ok, high_ok)):
        copy.wait_recv()
        fill(m, 1 - k, ok)

    across = (zlow + zpos) % 2
    half = HALF * ny
    tail_lane = lax.broadcasted_iota(jnp.int32, (half, 128), 1)
    tail_row = lax.broadcasted_iota(jnp.int32, (half, 128), 0)
    later = []
    for dz in range(2):
        for copy in w_far if dz else w_near:
            copy.wait_recv()
        part = slice(half * dz, half * dz + half)
        tail = wg[0, part, LAST:PADDED].astype(F32)
        with_bias = (tail_lane == DEPTH - LAST) & (tail_row // HALF == xpos) & (across == dz)
        chunk_bias = jnp.sum(jnp.where(with_bias, tail, 0.0), axis=1, keepdims=True)
        other_low = (across + dz) % 2
        for p in (1, 0):
            plane = flip(zpos, p)
            taps = rows(VIEWS * plane, DEPTH)
            ypart[plane, part, :] = (
                jnp.dot(wg[0, part, 0:DEPTH], xcol[0, taps, :], preferred_element_type=F32)
                + jnp.dot(wg[1, part, 0:DEPTH], xcol[1, taps, :], preferred_element_type=F32)
                + chunk_bias
            ).astype(BF16)
            for dx in steps:
                to = 2 * around(xpos + dx) + flip(zpos, dz)
                chunk = ypart.at[plane, place(around(xpos + dx), dz), :]
                copy = remote(
                    chunk, yrecv.at[2 * dx + other_low, half_rows(HALF * zpos), :],
                    y_send.at[2 * dx + dz, p], y_recv.at[2 * dx + other_low, p], 2 * to + k, 2 * ypos + plane,
                )
                if dx or p:
                    copy.start()
                    copies.append(copy)
                else:
                    away = other_low == 1

                    @pl.when(away)
                    def _():
                        copy.start()

                    @pl.when(jnp.logical_not(away))
                    def _():
                        yrecv[0, half_rows(HALF * zpos), :] = ypart[plane, place(xpos, dz), :]

                    later.append((away, copy))

    load_cot.wait()
    for dx, a, p in row_steps:
        if dx or a or p:
            arrived(yrecv.at[2 * dx + a, half_rows(HALF * flip(zpos, p)), :], y_recv.at[2 * dx + a, p])
    sectioned = yrecv[0].astype(F32)
    for j in range(1, nc):
        sectioned = sectioned + yrecv[j].astype(F32)
    s = 1.0 / (1.0 + jnp.exp(-sectioned))
    gown[...] = (cot[...].astype(F32) * (s * (1.0 + sectioned * (1.0 - s)))).astype(BF16)
    g_copies = []
    for dx, a, p in row_steps:
        part = half_rows(HALF * flip(zpos, p))
        rows_there = place(xpos, (across + p) % 2)
        if dx or a or p:
            g_copies.append(
                send(
                    gown.at[part, :], g.at[zpos, rows_there, :], g_send.at[2 * dx + a, p], g_recv.at[2 * dx + a, p],
                    2 * pair_at(dx, a) + k, 2 * ypos + flip(zpos, p),
                )
            )
        else:
            g[zpos, rows_there, :] = gown[part, :]

    out_v[...] = (sectioned * s).astype(BF16)
    store_out = pltpu.make_async_copy(out_v, out_hbm, store_sem.at[0])
    store_out.start()
    bsend[:, 0:CH] = lax.dot_general(jnp.ones((8, VOX), BF16), gown[...], NT, preferred_element_type=F32)
    b_copies = []
    for d in range(1, nc):
        b_copies.append(send(bsend, brecv.at[d], b_send.at[d], b_recv.at[d], row, (col + d) % nc))

    for copy in g_copies:
        copy.wait_recv()
    p_copies = []
    lands = half_rows(CH * k + HALF * zpos)
    for o in (1, 0):
        h = flip(k, o)
        total = jnp.zeros((2 * half, DEPTH), F32)
        for p in range(2):
            total = total + lax.dot_general(
                g[p], xcol[h, VIEWS * p : VIEWS * p + DEPTH, :], NT, preferred_element_type=F32
            )
        wgp[h, :, 0:DEPTH] = total.astype(BF16)
        for dy, dz in col_steps:
            part = place(around(ypos + dy), dz)
            if dy or dz or o:
                p_copies.append(
                    send(
                        wgp.at[h, part, :], wgrecv.at[dy, lands, :],
                        p_send.at[dy, dz, o], p_recv.at[dy, dz, o], sib if o else row, col_at(dy, dz),
                    )
                )
            else:
                wgrecv[0, lands, :] = wgp[h, part, :]

    def spread(h):
        for p in range(2):
            z[p] = lax.dot_general(wg[h], g[p], TN, preferred_element_type=F32)
        planes = []
        for m in range(4):
            total = jnp.zeros((CH, VOX), F32)
            for b in range(3):
                for c in range(3):
                    part = None
                    for p in range(2):
                        if 0 <= m - p <= 2:
                            start = VIEWS * (m - p) + CH * (3 * b + c)
                            term = z[p, start : start + CH, :]
                            part = term if part is None else part + term
                    total = total + moved_view(part, y, x, 1 - b, 1 - c)
            planes.append(total)
        return planes

    for m, total in enumerate(spread(1 - k)):
        dsib[m] = total.astype(BF16)
    d_copy = send(dsib, dsib_recv, d_send.at[0], d_recv.at[0], sib, col)
    for m, total in enumerate(spread(k)):
        dnear[m] = total
    d_copy.wait_recv()
    for m in range(4):
        dnear[m] = dnear[m] + dsib_recv[m].astype(F32)
    dfar[0] = dnear[0].astype(BF16)
    dfar[1] = dnear[2 - zpos].astype(BF16)
    dfar[2] = dnear[3].astype(BF16)
    send(dfar.at[0], dfar_recv.at[1 + zpos], h_send.at[0], h_recv.at[1 + zpos], row, 2 * around(ypos - 1) + 1)
    send(dfar.at[1], dfar_recv.at[0], h_send.at[1], h_recv.at[0], row, pair)
    send(dfar.at[2], dfar_recv.at[1 + zpos], h_send.at[2], h_recv.at[1 + zpos], row, 2 * around(ypos + 1))

    for copy in b_copies:
        copy.wait_recv()
    bias_sum = bsend[...]
    for d in range(1, nc):
        bias_sum = bias_sum + brecv[d]
    bsum_v[...] = bias_sum * norm_factor
    store_bias = pltpu.make_async_copy(bsum_v, bsum_hbm, store_sem.at[3])
    store_bias.start()

    for i in range(3):
        arrived(dfar_recv.at[i], h_recv.at[i])
    cross_ok = jnp.where(zpos == 1, high_ok, low_ok)
    near_sum = dnear[1 + zpos] + dfar_recv[0].astype(F32)
    near_sum = near_sum + cross_ok * (dfar_recv[1].astype(F32) + dfar_recv[2].astype(F32))
    dgrad_v[...] = near_sum.astype(BF16)
    store_data = pltpu.make_async_copy(dgrad_v, dgrad_hbm, store_sem.at[1])
    store_data.start()

    for copy in p_copies:
        copy.wait_recv()
    total = wgrecv[0].astype(F32)
    for d in range(1, ny):
        total = total + wgrecv[d].astype(F32)
    wsum_v[...] = total * norm_factor
    store_weights = pltpu.make_async_copy(wsum_v, wsum_hbm, store_sem.at[2])
    store_weights.start()

    for copy in copies:
        copy.wait_send()
    for sent, copy in later:

        @pl.when(sent)
        def _():
            copy.wait_send()

    for store in (store_out, store_data, store_weights, store_bias):
        store.wait()


def finish(
    out_in, dgrad_in, wsum_in, bsum_in, out_hbm, dgrad_hbm, wgrad_hbm, bgrad_hbm,
    out_v, dgrad_v, wsum_v, bsum_v, wgrad_v, bgrad_v, load_sem, store_sem,
):
    cut = (TAPS + 1) // 2 // 4 * 4 + 4
    lanes = (slice(0, CH * cut), slice(CH * cut, PADDED))
    taps = (slice(0, cut), slice(cut, TAPS))
    loads = [pltpu.make_async_copy(wsum_in.at[:, lanes[i]], wsum_v.at[:, lanes[i]], load_sem.at[i]) for i in range(2)]
    stores = [pltpu.make_async_copy(wgrad_v.at[taps[i]], wgrad_hbm.at[taps[i]], store_sem.at[i]) for i in range(2)]
    small = ((out_in, out_v, out_hbm), (dgrad_in, dgrad_v, dgrad_hbm), (bsum_in, bsum_v, None))
    for i, (src, dst, _) in enumerate(small):
        loads.append(pltpu.make_async_copy(src, dst, load_sem.at[2 + i]))
    for load in loads:
        load.start()
    for i in range(2):
        loads[i].wait()
        part = jnp.transpose(wsum_v[:, lanes[i]])
        count = taps[i].stop - taps[i].start
        wgrad_v[taps[i]] = part[0 : CH * count].reshape(count, CH, 2 * CH)
        stores[i].start()
    for i, (_, src, dst) in enumerate(small[:2]):
        loads[2 + i].wait()
        stores.append(pltpu.make_async_copy(src, dst, store_sem.at[2 + i]))
        stores[-1].start()
    loads[4].wait()
    bgrad_v[...] = bsum_v[0:1, 0:CH]
    stores.append(pltpu.make_async_copy(bgrad_v, bgrad_hbm, store_sem.at[4]))
    stores[-1].start()
    for store in stores:
        store.wait()


def on_device(nc, volume, filters, bias, cotangent):
    ny = nc // 2
    chunk = HALF * nc
    dma = pltpu.SemaphoreType.DMA
    hbm = pl.BlockSpec(memory_space=pl.ANY)
    plane = (CH, VOX)
    sums = pl.pallas_call(
        functools.partial(kernel, nc, 1.0 / math.sqrt(nc * VOX)),
        out_shape=(
            jax.ShapeDtypeStruct(plane, BF16),
            jax.ShapeDtypeStruct(plane, BF16),
            jax.ShapeDtypeStruct((2 * CH, PADDED), F32),
            jax.ShapeDtypeStruct((8, 128), F32),
        ),
        in_specs=[hbm] * 4,
        out_specs=(hbm,) * 4,
        scratch_shapes=[
            pltpu.VMEM((TAPS, CH, 2 * CH), BF16),
            pltpu.VMEM((1, 2 * CH), BF16),
            pltpu.VMEM(plane, BF16),
            pltpu.VMEM((PADDED, 128), F32),
            pltpu.VMEM((2 * CH, PADDED), BF16),
            pltpu.VMEM((2, chunk, PADDED), BF16),
            pltpu.VMEM((4, 2 * CH, VOX), BF16),
            pltpu.VMEM((2, 4 * VIEWS, VOX), BF16),
            pltpu.VMEM((2, chunk, VOX), BF16),
            pltpu.VMEM((nc, CH, VOX), BF16),
            pltpu.VMEM(plane, BF16),
            pltpu.VMEM((2, chunk, VOX), BF16),
            pltpu.VMEM((2, chunk, PADDED), BF16),
            pltpu.VMEM((ny, 2 * CH, PADDED), BF16),
            pltpu.VMEM((8, 128), F32),
            pltpu.VMEM((nc, 8, 128), F32),
            pltpu.VMEM((2, PADDED, VOX), F32),
            pltpu.VMEM((4, CH, VOX), BF16),
            pltpu.VMEM((4, CH, VOX), BF16),
            pltpu.VMEM((4, CH, VOX), F32),
            pltpu.VMEM((3, CH, VOX), BF16),
            pltpu.VMEM((3, CH, VOX), BF16),
            pltpu.VMEM(plane, BF16),
            pltpu.VMEM(plane, BF16),
            pltpu.VMEM((2 * CH, PADDED), F32),
            pltpu.VMEM((8, 128), F32),
            dma((4,)), dma((4,)),
            dma((3,)), dma((3,)), dma((4,)), dma((4,)),
            dma((ny, 2, 2)), dma((ny, 2, 2)),
            dma((nc, 2)), dma((nc, 2)), dma((nc, 2)), dma((nc, 2)), dma((nc,)), dma((nc,)),
            dma((ny, 2, 2)), dma((ny, 2, 2)), dma((1,)), dma((1,)), dma((3,)), dma((3,)),
        ],
        compiler_params=pltpu.CompilerParams(
            collective_id=0, has_side_effects=True, vmem_limit_bytes=VMEM_LIMIT
        ),
    )(volume, filters, bias.reshape(1, 2 * CH), cotangent)
    output, data_grad, weight_grad, bias_grad = pl.pallas_call(
        finish,
        out_shape=(
            jax.ShapeDtypeStruct(plane, BF16),
            jax.ShapeDtypeStruct(plane, BF16),
            jax.ShapeDtypeStruct((TAPS, CH, 2 * CH), F32),
            jax.ShapeDtypeStruct((1, CH), F32),
        ),
        in_specs=[hbm] * 4,
        out_specs=(hbm,) * 4,
        scratch_shapes=[
            pltpu.VMEM(plane, BF16),
            pltpu.VMEM(plane, BF16),
            pltpu.VMEM((2 * CH, PADDED), F32),
            pltpu.VMEM((8, 128), F32),
            pltpu.VMEM((TAPS, CH, 2 * CH), F32),
            pltpu.VMEM((1, CH), F32),
            dma((5,)), dma((5,)),
        ],
        compiler_params=pltpu.CompilerParams(vmem_limit_bytes=VMEM_LIMIT),
    )(*sums)
    return output, data_grad, weight_grad, bias_grad.reshape(CH)


def solution(mesh):
    placed = (P("row", "col"), P(None, "row", "col"), P("col"), P("row", "col"))
    return jax.shard_map(
        functools.partial(on_device, mesh.shape["col"]),
        mesh=mesh,
        in_specs=placed,
        out_specs=(P("row", "col"), P("row", "col"), P(None, "row", "col"), P("row")),
        check_vma=False,
    )
```

```python
import functools
import math

import jax
import jax.numpy as jnp
from jax import lax
from jax.experimental import pallas as pl
from jax.experimental.pallas import tpu as pltpu
from jax.sharding import PartitionSpec as P

S = 32
VOX = S * S
CH = 32
TAPS = 27
DEPTH = TAPS * CH
HALF = CH // 2
VIEWS = 9 * CH
PADDED = 896
LAST = PADDED - 128
MESH = pl.DeviceIdType.MESH
BF16 = jnp.bfloat16
F32 = jnp.float32
VMEM_LIMIT = 56 * 1024 * 1024
NT = (((1,), (1,)), ((), ()))
TN = (((0,), (0,)), ((), ()))


def inside(coord, step):
    moved = coord + step
    return (moved >= 0) & (moved < S)


def moved_view(value, y, x, dy, dx):
    offset = dy * S + dx
    if offset:
        value = pltpu.roll(value, (-offset) % VOX, 1)
    if dy or dx:
        value = jnp.where(inside(y, dy) & inside(x, dx), value, 0.0)
    return value


def kernel(
    nc, norm_factor,
    vol_hbm, w_hbm, bias_hbm, cot_hbm,
    out_hbm, dgrad_hbm, wsum_hbm, bsum_hbm,
    w_own, bias_own, cot, wpad, wt_own, wg, xin, xcol, ypart, yrecv, gown, g, wgp, wgrecv, bsend, brecv,
    z, dsib, dsib_recv, dnear, dfar, dfar_recv, out_v, dgrad_v, wsum_v, bsum_v,
    load_sem, store_sem, x_send, x_recv, xs_send, xs_recv, w_send, w_recv,
    y_send, y_recv, g_send, g_recv, b_send, b_recv, p_send, p_recv, d_send, d_recv, h_send, h_recv,
):
    row = lax.axis_index("row")
    col = lax.axis_index("col")
    q = row // 2
    k = row % 2
    sib = 2 * q + 1 - k
    ny = nc // 2
    xpos = q // 2
    zlow = q % 2
    ypos = col // 2
    zpos = col % 2
    pair = 2 * ypos + 1 - zpos

    def rows(start, size=CH):
        return pl.ds(pl.multiple_of(start, CH), size)

    def around(position):
        return (position + 2 * ny) % ny

    def half_rows(start):
        return pl.ds(pl.multiple_of(start, HALF), HALF)

    def flip(position, other_one):
        return 1 - position if other_one else position

    steps = [dx for dx in (1, 3, 2, 0) if dx < ny]
    col_steps = [(dy, dz) for dy in steps for dz in (1, 0)]
    row_steps = [(dx, a, p) for a in (0, 1) for p in (0, 1) for dx in steps]

    def col_at(dy, dz):
        return 2 * around(ypos + dy) + flip(zpos, dz)

    def pair_at(dx, a):
        return 2 * around(xpos + dx) + flip(zlow, a)

    def place(along, half):
        return half_rows(HALF * (ny * half + along))

    def remote(src, dst, send_sem, recv_sem, to_row, to_col):
        return pltpu.make_async_remote_copy(
            src_ref=src, dst_ref=dst, send_sem=send_sem, recv_sem=recv_sem,
            device_id=(to_row, to_col), device_id_type=MESH,
        )

    copies = []

    def send(*args):
        copy = remote(*args)
        copy.start()
        copies.append(copy)
        return copy

    def arrived(dst, sem):
        remote(dst, dst, sem, sem, sib, col).wait_recv()

    load_w = pltpu.make_async_copy(w_hbm, w_own, load_sem.at[0])
    load_bias = pltpu.make_async_copy(bias_hbm, bias_own, load_sem.at[1])
    mine, other = rows(CH * k), rows(CH * (1 - k))
    load_vol = pltpu.make_async_copy(vol_hbm, xin.at[1 + zpos, mine, :], load_sem.at[2])
    load_cot = pltpu.make_async_copy(cot_hbm, cot, load_sem.at[3])
    for load in (load_w, load_bias, load_vol, load_cot):
        load.start()

    barrier = pltpu.get_barrier_semaphore()
    peers = [(sib if o else row, col_at(dy, dz)) for dy, dz in col_steps for o in range(2) if dy or dz or o]
    peers += [(2 * pair_at(dx, a) + k, 2 * ypos + flip(zpos, p)) for dx, a, p in row_steps if dx or a or p]
    for peer in peers:
        pl.semaphore_signal(barrier, inc=1, device_id=peer, device_id_type=MESH)

    wpad[...] = jnp.zeros_like(wpad)
    bsend[...] = jnp.zeros_like(bsend)
    wgp[:, :, LAST:PADDED] = jnp.zeros((2, HALF * nc, 128), BF16)
    load_vol.wait()

    pl.semaphore_wait(barrier, len(peers))

    own_plane = xin.at[1 + zpos, mine, :]
    side = 2 * around(ypos + 2 * zpos - 1)
    edge = xin.at[3 - 3 * zpos, mine, :]
    for i in range(2):
        send(own_plane, edge, x_send.at[1 + i], x_recv.at[2 - zpos], row, side + flip(zpos, 1 - i))
    x_sib = send(own_plane, own_plane, xs_send.at[0], xs_recv.at[0], sib, col)
    x_pair = send(own_plane, own_plane, x_send.at[0], x_recv.at[0], row, pair)

    load_w.wait()
    load_bias.wait()
    wpad[0:DEPTH, 0 : 2 * CH] = w_own[...].reshape(DEPTH, 2 * CH).astype(F32)
    wpad[DEPTH : DEPTH + 1, 0 : 2 * CH] = bias_own[...].astype(F32)
    wt_own[...] = jnp.transpose(wpad[...])[0 : 2 * CH].astype(BF16)

    w_near, w_far = [], []
    for dz in range(2):
        for dy in (*steps[-1:], *steps[:-1]):
            for o in (1, 0):
                if dy or dz or o:
                    part = half_rows(CH * flip(k, o) + HALF * flip(zpos, dz))
                    (w_far if dz else w_near).append(
                        send(
                            wt_own.at[part, :], wg.at[k, place(ypos, dz), :],
                            w_send.at[dy, dz, o], w_recv.at[dy, dz, o], sib if o else row, col_at(dy, dz),
                        )
                    )
    wg[k, place(ypos, 0), :] = wt_own[half_rows(CH * k + HALF * zpos), :]

    lane = lax.broadcasted_iota(jnp.int32, (CH, VOX), 1)
    y, x = lane // S, lane % S
    low_ok = (ypos > 0).astype(F32)
    high_ok = (ypos < ny - 1).astype(F32)

    def fill(m, h, ok=None):
        plane = xin[m, rows(CH * h), :].astype(F32)
        if ok is not None:
            plane = plane * ok
        for b in range(3):
            for c in range(3):
                start = VIEWS * m + CH * (3 * b + c)
                xcol[h, rows(start), :] = moved_view(plane, y, x, b - 1, c - 1).astype(BF16)

    fill(1 + zpos, k)
    x_sib.wait_recv()
    fill(1 + zpos, 1 - k)
    to_sib = []
    for i, m in ((0, 2 - zpos), (1, 0), (2, 3)):
        part = xin.at[m, mine, :]
        arrived(part, x_recv.at[i])
        to_sib.append(send(part, part, xs_send.at[1 + i], xs_recv.at[1 + i], sib, col))
    fill(2 - zpos, k)
    fill(0, k, low_ok)
    fill(3, k, high_ok)
    for copy, m, ok in zip(to_sib, (2 - zpos, 0, 3), (None, low_ok, high_ok)):
        copy.wait_recv()
        fill(m, 1 - k, ok)

    across = (zlow + zpos) % 2
    half = HALF * ny
    tail_lane = lax.broadcasted_iota(jnp.int32, (half, 128), 1)
    tail_row = lax.broadcasted_iota(jnp.int32, (half, 128), 0)
    later = []
    for dz in range(2):
        for copy in w_far if dz else w_near:
            copy.wait_recv()
        part = slice(half * dz, half * dz + half)
        tail = wg[0, part, LAST:PADDED].astype(F32)
        with_bias = (tail_lane == DEPTH - LAST) & (tail_row // HALF == xpos) & (across == dz)
        chunk_bias = jnp.sum(jnp.where(with_bias, tail, 0.0), axis=1, keepdims=True)
        other_low = (across + dz) % 2
        for p in (1, 0):
            plane = flip(zpos, p)
            taps = rows(VIEWS * plane, DEPTH)
            ypart[plane, part, :] = (
                jnp.dot(wg[0, part, 0:DEPTH], xcol[0, taps, :], preferred_element_type=F32)
                + jnp.dot(wg[1, part, 0:DEPTH], xcol[1, taps, :], preferred_element_type=F32)
                + chunk_bias
            ).astype(BF16)
            for dx in steps:
                to = 2 * around(xpos + dx) + flip(zpos, dz)
                chunk = ypart.at[plane, place(around(xpos + dx), dz), :]
                copy = remote(
                    chunk, yrecv.at[2 * dx + other_low, half_rows(HALF * zpos), :],
                    y_send.at[2 * dx + dz, p], y_recv.at[2 * dx + other_low, p], 2 * to + k, 2 * ypos + plane,
                )
                if dx or p:
                    copy.start()
                    copies.append(copy)
                else:
                    away = other_low == 1

                    @pl.when(away)
                    def _():
                        copy.start()

                    @pl.when(jnp.logical_not(away))
                    def _():
                        yrecv[0, half_rows(HALF * zpos), :] = ypart[plane, place(xpos, dz), :]

                    later.append((away, copy))

    load_cot.wait()
    for dx, a, p in row_steps:
        if dx or a or p:
            arrived(yrecv.at[2 * dx + a, half_rows(HALF * flip(zpos, p)), :], y_recv.at[2 * dx + a, p])
    sectioned = yrecv[0].astype(F32)
    for j in range(1, nc):
        sectioned = sectioned + yrecv[j].astype(F32)
    s = 1.0 / (1.0 + jnp.exp(-sectioned))
    gown[...] = (cot[...].astype(F32) * (s * (1.0 + sectioned * (1.0 - s)))).astype(BF16)
    g_copies = []
    for dx, a, p in row_steps:
        part = half_rows(HALF * flip(zpos, p))
        rows_there = place(xpos, (across + p) % 2)
        if dx or a or p:
            g_copies.append(
                send(
                    gown.at[part, :], g.at[zpos, rows_there, :], g_send.at[2 * dx + a, p], g_recv.at[2 * dx + a, p],
                    2 * pair_at(dx, a) + k, 2 * ypos + flip(zpos, p),
                )
            )
        else:
            g[zpos, rows_there, :] = gown[part, :]

    out_v[...] = (sectioned * s).astype(BF16)
    store_out = pltpu.make_async_copy(out_v, out_hbm, store_sem.at[0])
    store_out.start()
    bsend[:, 0:CH] = lax.dot_general(jnp.ones((8, VOX), BF16), gown[...], NT, preferred_element_type=F32)
    b_copies = []
    for d in range(1, nc):
        b_copies.append(send(bsend, brecv.at[d], b_send.at[d], b_recv.at[d], row, (col + d) % nc))

    for copy in g_copies:
        copy.wait_recv()
    early = list(copies)
    p_copies = ([], [])
    lands = half_rows(CH * k + HALF * zpos)
    for o in (1, 0):
        h = flip(k, o)
        total = jnp.zeros((2 * half, DEPTH), F32)
        for p in range(2):
            total = total + lax.dot_general(
                g[p], xcol[h, VIEWS * p : VIEWS * p + DEPTH, :], NT, preferred_element_type=F32
            )
        wgp[h, :, 0:DEPTH] = total.astype(BF16)
        for dy, dz in col_steps:
            part = place(around(ypos + dy), dz)
            if dy or dz or o:
                p_copies[o].append(
                    send(
                        wgp.at[h, part, :], wgrecv.at[dy, lands, :],
                        p_send.at[dy, dz, o], p_recv.at[dy, dz, o], sib if o else row, col_at(dy, dz),
                    )
                )
            else:
                wgrecv[0, lands, :] = wgp[h, part, :]

    def products(h):
        for p in range(2):
            z[p] = lax.dot_general(wg[h], g[p], TN, preferred_element_type=F32)

    def spread(m):
        total = jnp.zeros((CH, VOX), F32)
        for b in range(3):
            for c in range(3):
                part = None
                for p in range(2):
                    if 0 <= m - p <= 2:
                        start = VIEWS * (m - p) + CH * (3 * b + c)
                        term = z[p, start : start + CH, :]
                        part = term if part is None else part + term
                total = total + moved_view(part, y, x, 1 - b, 1 - c)
        return total

    def send_far(slot, value, land, to_col):
        dfar[slot] = value.astype(BF16)
        send(dfar.at[slot], dfar_recv.at[land], h_send.at[slot], h_recv.at[land], row, to_col)

    products(1 - k)
    d_copies = {}
    for m in (0, 3, 1, 2):
        dsib[m] = spread(m).astype(BF16)
        d_copies[m] = send(dsib.at[m], dsib_recv.at[m], d_send.at[m], d_recv.at[m], sib, col)
    products(k)
    for m in (0, 3, 1, 2):
        total = spread(m)
        d_copies[m].wait_recv()
        total = total + dsib_recv[m].astype(F32)
        if m == 0:
            send_far(0, total, 1 + zpos, 2 * around(ypos - 1) + 1)
        elif m == 3:
            send_far(2, total, 1 + zpos, 2 * around(ypos + 1))
        else:
            dnear[m] = total
    send_far(1, dnear[2 - zpos], 0, pair)

    for copy in early:
        copy.wait_send()
    for sent, copy in later:

        @pl.when(sent)
        def _():
            copy.wait_send()

    for copy in b_copies:
        copy.wait_recv()
    bias_sum = bsend[...]
    for d in range(1, nc):
        bias_sum = bias_sum + brecv[d]
    bsum_v[...] = bias_sum * norm_factor
    store_bias = pltpu.make_async_copy(bsum_v, bsum_hbm, store_sem.at[3])
    store_bias.start()

    stores = [store_out, store_bias]
    for o in (1, 0):
        for copy in p_copies[o]:
            copy.wait_recv()
        part = other if o else mine
        total = wgrecv[0, part, :].astype(F32)
        for dy in range(1, ny):
            total = total + wgrecv[dy, part, :].astype(F32)
        wsum_v[part, :] = total * norm_factor
        stores.append(pltpu.make_async_copy(wsum_v.at[part, :], wsum_hbm.at[part, :], store_sem.at[4 if o else 2]))
        stores[-1].start()

    for i in range(3):
        arrived(dfar_recv.at[i], h_recv.at[i])
    cross_ok = jnp.where(zpos == 1, high_ok, low_ok)
    near_sum = dnear[1 + zpos] + dfar_recv[0].astype(F32)
    near_sum = near_sum + cross_ok * (dfar_recv[1].astype(F32) + dfar_recv[2].astype(F32))
    dgrad_v[...] = near_sum.astype(BF16)
    store_data = pltpu.make_async_copy(dgrad_v, dgrad_hbm, store_sem.at[1])
    store_data.start()

    for copy in copies[len(early) :]:
        copy.wait_send()
    for store in (*stores, store_data):
        store.wait()


def finish(
    out_in, dgrad_in, wsum_in, bsum_in, out_hbm, dgrad_hbm, wgrad_hbm, bgrad_hbm,
    out_v, dgrad_v, wsum_v, bsum_v, wgrad_v, bgrad_v, load_sem, store_sem,
):
    cut = (TAPS + 1) // 2 // 4 * 4 + 4
    lanes = (slice(0, CH * cut), slice(CH * cut, PADDED))
    taps = (slice(0, cut), slice(cut, TAPS))
    loads = [pltpu.make_async_copy(wsum_in.at[:, lanes[i]], wsum_v.at[:, lanes[i]], load_sem.at[i]) for i in range(2)]
    stores = [pltpu.make_async_copy(wgrad_v.at[taps[i]], wgrad_hbm.at[taps[i]], store_sem.at[i]) for i in range(2)]
    small = ((out_in, out_v, out_hbm), (dgrad_in, dgrad_v, dgrad_hbm), (bsum_in, bsum_v, None))
    for i, (src, dst, _) in enumerate(small):
        loads.append(pltpu.make_async_copy(src, dst, load_sem.at[2 + i]))
    for load in loads:
        load.start()
    for i in range(2):
        loads[i].wait()
        part = jnp.transpose(wsum_v[:, lanes[i]])
        count = taps[i].stop - taps[i].start
        wgrad_v[taps[i]] = part[0 : CH * count].reshape(count, CH, 2 * CH)
        stores[i].start()
    for i, (_, src, dst) in enumerate(small[:2]):
        loads[2 + i].wait()
        stores.append(pltpu.make_async_copy(src, dst, store_sem.at[2 + i]))
        stores[-1].start()
    loads[4].wait()
    bgrad_v[...] = bsum_v[0:1, 0:CH]
    stores.append(pltpu.make_async_copy(bgrad_v, bgrad_hbm, store_sem.at[4]))
    stores[-1].start()
    for store in stores:
        store.wait()


def on_device(nc, volume, filters, bias, cotangent):
    ny = nc // 2
    chunk = HALF * nc
    dma = pltpu.SemaphoreType.DMA
    hbm = pl.BlockSpec(memory_space=pl.ANY)
    plane = (CH, VOX)
    sums = pl.pallas_call(
        functools.partial(kernel, nc, 1.0 / math.sqrt(nc * VOX)),
        out_shape=(
            jax.ShapeDtypeStruct(plane, BF16),
            jax.ShapeDtypeStruct(plane, BF16),
            jax.ShapeDtypeStruct((2 * CH, PADDED), F32),
            jax.ShapeDtypeStruct((8, 128), F32),
        ),
        in_specs=[hbm] * 4,
        out_specs=(hbm,) * 4,
        scratch_shapes=[
            pltpu.VMEM((TAPS, CH, 2 * CH), BF16),
            pltpu.VMEM((1, 2 * CH), BF16),
            pltpu.VMEM(plane, BF16),
            pltpu.VMEM((PADDED, 128), F32),
            pltpu.VMEM((2 * CH, PADDED), BF16),
            pltpu.VMEM((2, chunk, PADDED), BF16),
            pltpu.VMEM((4, 2 * CH, VOX), BF16),
            pltpu.VMEM((2, 4 * VIEWS, VOX), BF16),
            pltpu.VMEM((2, chunk, VOX), BF16),
            pltpu.VMEM((nc, CH, VOX), BF16),
            pltpu.VMEM(plane, BF16),
            pltpu.VMEM((2, chunk, VOX), BF16),
            pltpu.VMEM((2, chunk, PADDED), BF16),
            pltpu.VMEM((ny, 2 * CH, PADDED), BF16),
            pltpu.VMEM((8, 128), F32),
            pltpu.VMEM((nc, 8, 128), F32),
            pltpu.VMEM((2, PADDED, VOX), F32),
            pltpu.VMEM((4, CH, VOX), BF16),
            pltpu.VMEM((4, CH, VOX), BF16),
            pltpu.VMEM((4, CH, VOX), F32),
            pltpu.VMEM((3, CH, VOX), BF16),
            pltpu.VMEM((3, CH, VOX), BF16),
            pltpu.VMEM(plane, BF16),
            pltpu.VMEM(plane, BF16),
            pltpu.VMEM((2 * CH, PADDED), F32),
            pltpu.VMEM((8, 128), F32),
            dma((4,)), dma((5,)),
            dma((3,)), dma((3,)), dma((4,)), dma((4,)),
            dma((ny, 2, 2)), dma((ny, 2, 2)),
            dma((nc, 2)), dma((nc, 2)), dma((nc, 2)), dma((nc, 2)), dma((nc,)), dma((nc,)),
            dma((ny, 2, 2)), dma((ny, 2, 2)), dma((4,)), dma((4,)), dma((3,)), dma((3,)),
        ],
        compiler_params=pltpu.CompilerParams(
            collective_id=0, has_side_effects=True, vmem_limit_bytes=VMEM_LIMIT
        ),
    )(volume, filters, bias.reshape(1, 2 * CH), cotangent)
    output, data_grad, weight_grad, bias_grad = pl.pallas_call(
        finish,
        out_shape=(
            jax.ShapeDtypeStruct(plane, BF16),
            jax.ShapeDtypeStruct(plane, BF16),
            jax.ShapeDtypeStruct((TAPS, CH, 2 * CH), F32),
            jax.ShapeDtypeStruct((1, CH), F32),
        ),
        in_specs=[hbm] * 4,
        out_specs=(hbm,) * 4,
        scratch_shapes=[
            pltpu.VMEM(plane, BF16),
            pltpu.VMEM(plane, BF16),
            pltpu.VMEM((2 * CH, PADDED), F32),
            pltpu.VMEM((8, 128), F32),
            pltpu.VMEM((TAPS, CH, 2 * CH), F32),
            pltpu.VMEM((1, CH), F32),
            dma((5,)), dma((5,)),
        ],
        compiler_params=pltpu.CompilerParams(vmem_limit_bytes=VMEM_LIMIT),
    )(*sums)
    return output, data_grad, weight_grad, bias_grad.reshape(CH)


def solution(mesh):
    placed = (P("row", "col"), P(None, "row", "col"), P("col"), P("row", "col"))
    return jax.shard_map(
        functools.partial(on_device, mesh.shape["col"]),
        mesh=mesh,
        in_specs=placed,
        out_specs=(P("row", "col"), P("row", "col"), P(None, "row", "col"), P("row")),
        check_vma=False,
    )
```

```python
import functools
import math

import jax
import jax.numpy as jnp
from jax import lax
from jax.experimental import pallas as pl
from jax.experimental.pallas import tpu as pltpu
from jax.sharding import PartitionSpec as P

S = 32
VOX = S * S
CH = 32
TAPS = 27
DEPTH = TAPS * CH
HALF = CH // 2
VIEWS = 9 * CH
PADDED = 896
LAST = PADDED - 128
MESH = pl.DeviceIdType.MESH
BF16 = jnp.bfloat16
F32 = jnp.float32
VMEM_LIMIT = 56 * 1024 * 1024
NT = (((1,), (1,)), ((), ()))
TN = (((0,), (0,)), ((), ()))


def inside(coord, step):
    moved = coord + step
    return (moved >= 0) & (moved < S)


def moved_view(value, y, x, dy, dx):
    offset = dy * S + dx
    if offset:
        value = pltpu.roll(value, (-offset) % VOX, 1)
    if dy or dx:
        value = jnp.where(inside(y, dy) & inside(x, dx), value, 0.0)
    return value


def kernel(
    nc, norm_factor,
    vol_hbm, w_hbm, bias_hbm, cot_hbm,
    out_hbm, dgrad_hbm, wsum_hbm, bsum_hbm,
    w_own, bias_own, cot, wpad, wt_own, wg, xin, xcol, ypart, yrecv, gown, g, wgp, wgrecv, bsend, brecv,
    z, dsib, dsib_recv, dnear, dfar, dfar_recv, out_v, dgrad_v, wsum_v, bsum_v,
    load_sem, store_sem, x_send, x_recv, xs_send, xs_recv, w_send, w_recv,
    y_send, y_recv, g_send, g_recv, b_send, b_recv, p_send, p_recv, d_send, d_recv, h_send, h_recv,
):
    row = lax.axis_index("row")
    col = lax.axis_index("col")
    q = row // 2
    k = row % 2
    sib = 2 * q + 1 - k
    ny = nc // 2
    xpos = q // 2
    zlow = q % 2
    ypos = col // 2
    zpos = col % 2
    pair = 2 * ypos + 1 - zpos

    def rows(start, size=CH):
        return pl.ds(pl.multiple_of(start, CH), size)

    def around(position):
        return (position + 2 * ny) % ny

    def half_rows(start):
        return pl.ds(pl.multiple_of(start, HALF), HALF)

    def flip(position, other_one):
        return 1 - position if other_one else position

    steps = [dx for dx in (1, 3, 2, 0) if dx < ny]
    col_steps = [(dy, dz) for dy in steps for dz in (1, 0)]
    row_steps = [(dx, a, p) for a in (0, 1) for p in (0, 1) for dx in steps]

    def col_at(dy, dz):
        return 2 * around(ypos + dy) + flip(zpos, dz)

    def pair_at(dx, a):
        return 2 * around(xpos + dx) + flip(zlow, a)

    def place(along, half):
        return half_rows(HALF * (ny * half + along))

    def remote(src, dst, send_sem, recv_sem, to_row, to_col):
        return pltpu.make_async_remote_copy(
            src_ref=src, dst_ref=dst, send_sem=send_sem, recv_sem=recv_sem,
            device_id=(to_row, to_col), device_id_type=MESH,
        )

    copies = []

    def send(*args):
        copy = remote(*args)
        copy.start()
        copies.append(copy)
        return copy

    def arrived(dst, sem):
        remote(dst, dst, sem, sem, sib, col).wait_recv()

    load_w = pltpu.make_async_copy(w_hbm, w_own, load_sem.at[0])
    load_bias = pltpu.make_async_copy(bias_hbm, bias_own, load_sem.at[1])
    mine, other = rows(CH * k), rows(CH * (1 - k))
    load_vol = pltpu.make_async_copy(vol_hbm, xin.at[1 + zpos, mine, :], load_sem.at[2])
    load_cot = pltpu.make_async_copy(cot_hbm, cot, load_sem.at[3])
    load_vol.start()

    barrier = pltpu.get_barrier_semaphore()
    peers = [(sib if o else row, col_at(dy, dz)) for dy, dz in col_steps for o in range(2) if dy or dz or o]
    peers += [(2 * pair_at(dx, a) + k, 2 * ypos + flip(zpos, p)) for dx, a, p in row_steps if dx or a or p]
    for peer in peers:
        pl.semaphore_signal(barrier, inc=1, device_id=peer, device_id_type=MESH)
    for load in (load_w, load_bias, load_cot):
        load.start()

    wpad[...] = jnp.zeros_like(wpad)
    bsend[...] = jnp.zeros_like(bsend)
    wgp[:, :, LAST:PADDED] = jnp.zeros((2, HALF * nc, 128), BF16)
    load_vol.wait()

    pl.semaphore_wait(barrier, len(peers))

    own_plane = xin.at[1 + zpos, mine, :]
    side = 2 * around(ypos + 2 * zpos - 1)
    edge = xin.at[3 - 3 * zpos, mine, :]
    for i in range(2):
        send(own_plane, edge, x_send.at[1 + i], x_recv.at[2 - zpos], row, side + flip(zpos, 1 - i))
    x_sib = send(own_plane, own_plane, xs_send.at[0], xs_recv.at[0], sib, col)
    x_pair = send(own_plane, own_plane, x_send.at[0], x_recv.at[0], row, pair)

    load_w.wait()
    load_bias.wait()
    wpad[0:DEPTH, 0 : 2 * CH] = w_own[...].reshape(DEPTH, 2 * CH).astype(F32)
    wpad[DEPTH : DEPTH + 1, 0 : 2 * CH] = bias_own[...].astype(F32)
    wt_own[...] = jnp.transpose(wpad[...])[0 : 2 * CH].astype(BF16)

    w_near, w_far = [], []
    for dz in range(2):
        for dy in (*steps[-1:], *steps[:-1]):
            for o in (1, 0):
                if dy or dz or o:
                    part = half_rows(CH * flip(k, o) + HALF * flip(zpos, dz))
                    (w_far if dz else w_near).append(
                        send(
                            wt_own.at[part, :], wg.at[k, place(ypos, dz), :],
                            w_send.at[dy, dz, o], w_recv.at[dy, dz, o], sib if o else row, col_at(dy, dz),
                        )
                    )
    wg[k, place(ypos, 0), :] = wt_own[half_rows(CH * k + HALF * zpos), :]

    lane = lax.broadcasted_iota(jnp.int32, (CH, VOX), 1)
    y, x = lane // S, lane % S
    low_ok = (ypos > 0).astype(F32)
    high_ok = (ypos < ny - 1).astype(F32)

    def fill(m, h, ok=None):
        plane = xin[m, rows(CH * h), :].astype(F32)
        if ok is not None:
            plane = plane * ok
        for b in range(3):
            for c in range(3):
                start = VIEWS * m + CH * (3 * b + c)
                xcol[h, rows(start), :] = moved_view(plane, y, x, b - 1, c - 1).astype(BF16)

    fill(1 + zpos, k)
    x_sib.wait_recv()
    fill(1 + zpos, 1 - k)
    to_sib = []
    for i, m in ((0, 2 - zpos), (1, 0), (2, 3)):
        part = xin.at[m, mine, :]
        arrived(part, x_recv.at[i])
        to_sib.append(send(part, part, xs_send.at[1 + i], xs_recv.at[1 + i], sib, col))
    fill(2 - zpos, k)
    fill(0, k, low_ok)
    fill(3, k, high_ok)
    for copy, m, ok in zip(to_sib, (2 - zpos, 0, 3), (None, low_ok, high_ok)):
        copy.wait_recv()
        fill(m, 1 - k, ok)

    across = (zlow + zpos) % 2
    half = HALF * ny
    tail_lane = lax.broadcasted_iota(jnp.int32, (half, 128), 1)
    tail_row = lax.broadcasted_iota(jnp.int32, (half, 128), 0)
    later = []
    for dz in range(2):
        for copy in w_far if dz else w_near:
            copy.wait_recv()
        part = slice(half * dz, half * dz + half)
        tail = wg[0, part, LAST:PADDED].astype(F32)
        with_bias = (tail_lane == DEPTH - LAST) & (tail_row // HALF == xpos) & (across == dz)
        chunk_bias = jnp.sum(jnp.where(with_bias, tail, 0.0), axis=1, keepdims=True)
        other_low = (across + dz) % 2
        for p in (1, 0):
            plane = flip(zpos, p)
            taps = rows(VIEWS * plane, DEPTH)
            ypart[plane, part, :] = (
                jnp.dot(wg[0, part, 0:DEPTH], xcol[0, taps, :], preferred_element_type=F32)
                + jnp.dot(wg[1, part, 0:DEPTH], xcol[1, taps, :], preferred_element_type=F32)
                + chunk_bias
            ).astype(BF16)
            for dx in steps:
                to = 2 * around(xpos + dx) + flip(zpos, dz)
                chunk = ypart.at[plane, place(around(xpos + dx), dz), :]
                copy = remote(
                    chunk, yrecv.at[2 * dx + other_low, half_rows(HALF * zpos), :],
                    y_send.at[2 * dx + dz, p], y_recv.at[2 * dx + other_low, p], 2 * to + k, 2 * ypos + plane,
                )
                if dx or p:
                    copy.start()
                    copies.append(copy)
                else:
                    away = other_low == 1

                    @pl.when(away)
                    def _():
                        copy.start()

                    @pl.when(jnp.logical_not(away))
                    def _():
                        yrecv[0, half_rows(HALF * zpos), :] = ypart[plane, place(xpos, dz), :]

                    later.append((away, copy))

    load_cot.wait()
    for dx, a, p in row_steps:
        if dx or a or p:
            arrived(yrecv.at[2 * dx + a, half_rows(HALF * flip(zpos, p)), :], y_recv.at[2 * dx + a, p])
    sectioned = yrecv[0].astype(F32)
    for j in range(1, nc):
        sectioned = sectioned + yrecv[j].astype(F32)
    s = 1.0 / (1.0 + jnp.exp(-sectioned))
    gown[...] = (cot[...].astype(F32) * (s * (1.0 + sectioned * (1.0 - s)))).astype(BF16)
    g_copies = []
    for dx, a, p in row_steps:
        part = half_rows(HALF * flip(zpos, p))
        rows_there = place(xpos, (across + p) % 2)
        if dx or a or p:
            g_copies.append(
                send(
                    gown.at[part, :], g.at[zpos, rows_there, :], g_send.at[2 * dx + a, p], g_recv.at[2 * dx + a, p],
                    2 * pair_at(dx, a) + k, 2 * ypos + flip(zpos, p),
                )
            )
        else:
            g[zpos, rows_there, :] = gown[part, :]

    out_v[...] = (sectioned * s).astype(BF16)
    store_out = pltpu.make_async_copy(out_v, out_hbm, store_sem.at[0])
    store_out.start()
    bsend[:, 0:CH] = lax.dot_general(jnp.ones((8, VOX), BF16), gown[...], NT, preferred_element_type=F32)
    b_copies = []
    for d in range(1, nc):
        b_copies.append(send(bsend, brecv.at[d], b_send.at[d], b_recv.at[d], row, (col + d) % nc))

    for copy in g_copies:
        copy.wait_recv()
    early = list(copies)
    p_copies = ([], [])
    lands = half_rows(CH * k + HALF * zpos)
    for o in (1, 0):
        h = flip(k, o)
        total = jnp.zeros((2 * half, DEPTH), F32)
        for p in range(2):
            total = total + lax.dot_general(
                g[p], xcol[h, VIEWS * p : VIEWS * p + DEPTH, :], NT, preferred_element_type=F32
            )
        wgp[h, :, 0:DEPTH] = total.astype(BF16)
        for dy, dz in col_steps:
            part = place(around(ypos + dy), dz)
            if dy or dz or o:
                p_copies[o].append(
                    send(
                        wgp.at[h, part, :], wgrecv.at[dy, lands, :],
                        p_send.at[dy, dz, o], p_recv.at[dy, dz, o], sib if o else row, col_at(dy, dz),
                    )
                )
            else:
                wgrecv[0, lands, :] = wgp[h, part, :]

    def products(h):
        for p in range(2):
            z[p] = lax.dot_general(wg[h], g[p], TN, preferred_element_type=F32)

    def spread(m):
        total = jnp.zeros((CH, VOX), F32)
        for b in range(3):
            for c in range(3):
                part = None
                for p in range(2):
                    if 0 <= m - p <= 2:
                        start = VIEWS * (m - p) + CH * (3 * b + c)
                        term = z[p, start : start + CH, :]
                        part = term if part is None else part + term
                total = total + moved_view(part, y, x, 1 - b, 1 - c)
        return total

    def send_far(slot, value, land, to_col):
        dfar[slot] = value.astype(BF16)
        send(dfar.at[slot], dfar_recv.at[land], h_send.at[slot], h_recv.at[land], row, to_col)

    products(1 - k)
    d_copies = {}
    for m in (0, 3, 1, 2):
        dsib[m] = spread(m).astype(BF16)
        d_copies[m] = send(dsib.at[m], dsib_recv.at[m], d_send.at[m], d_recv.at[m], sib, col)
    products(k)
    for m in (0, 3, 1, 2):
        total = spread(m)
        d_copies[m].wait_recv()
        total = total + dsib_recv[m].astype(F32)
        if m == 0:
            send_far(0, total, 1 + zpos, 2 * around(ypos - 1) + 1)
        elif m == 3:
            send_far(2, total, 1 + zpos, 2 * around(ypos + 1))
        else:
            dnear[m] = total
    send_far(1, dnear[2 - zpos], 0, pair)

    for copy in early:
        copy.wait_send()
    for sent, copy in later:

        @pl.when(sent)
        def _():
            copy.wait_send()

    for copy in b_copies:
        copy.wait_recv()
    bias_sum = bsend[...]
    for d in range(1, nc):
        bias_sum = bias_sum + brecv[d]
    bsum_v[...] = bias_sum * norm_factor
    store_bias = pltpu.make_async_copy(bsum_v, bsum_hbm, store_sem.at[3])
    store_bias.start()

    stores = [store_out, store_bias]
    for o in (1, 0):
        for copy in p_copies[o]:
            copy.wait_recv()
        part = other if o else mine
        total = wgrecv[0, part, :].astype(F32)
        for dy in range(1, ny):
            total = total + wgrecv[dy, part, :].astype(F32)
        wsum_v[part, :] = total * norm_factor
        stores.append(pltpu.make_async_copy(wsum_v.at[part, :], wsum_hbm.at[part, :], store_sem.at[4 if o else 2]))
        stores[-1].start()

    for i in range(3):
        arrived(dfar_recv.at[i], h_recv.at[i])
    cross_ok = jnp.where(zpos == 1, high_ok, low_ok)
    near_sum = dnear[1 + zpos] + dfar_recv[0].astype(F32)
    near_sum = near_sum + cross_ok * (dfar_recv[1].astype(F32) + dfar_recv[2].astype(F32))
    dgrad_v[...] = near_sum.astype(BF16)
    store_data = pltpu.make_async_copy(dgrad_v, dgrad_hbm, store_sem.at[1])
    store_data.start()

    for copy in copies[len(early) :]:
        copy.wait_send()
    for store in (*stores, store_data):
        store.wait()


def finish(
    out_in, dgrad_in, wsum_in, bsum_in, out_hbm, dgrad_hbm, wgrad_hbm, bgrad_hbm,
    out_v, dgrad_v, wsum_v, bsum_v, wgrad_v, bgrad_v, load_sem, store_sem,
):
    cut = (TAPS + 1) // 2 // 4 * 4 + 4
    lanes = (slice(0, CH * cut), slice(CH * cut, PADDED))
    taps = (slice(0, cut), slice(cut, TAPS))
    loads = [pltpu.make_async_copy(wsum_in.at[:, lanes[i]], wsum_v.at[:, lanes[i]], load_sem.at[i]) for i in range(2)]
    stores = [pltpu.make_async_copy(wgrad_v.at[taps[i]], wgrad_hbm.at[taps[i]], store_sem.at[i]) for i in range(2)]
    small = ((out_in, out_v, out_hbm), (dgrad_in, dgrad_v, dgrad_hbm), (bsum_in, bsum_v, None))
    for i, (src, dst, _) in enumerate(small):
        loads.append(pltpu.make_async_copy(src, dst, load_sem.at[2 + i]))
    for load in loads:
        load.start()
    for i in range(2):
        loads[i].wait()
        part = jnp.transpose(wsum_v[:, lanes[i]])
        count = taps[i].stop - taps[i].start
        wgrad_v[taps[i]] = part[0 : CH * count].reshape(count, CH, 2 * CH)
        stores[i].start()
    for i, (_, src, dst) in enumerate(small[:2]):
        loads[2 + i].wait()
        stores.append(pltpu.make_async_copy(src, dst, store_sem.at[2 + i]))
        stores[-1].start()
    loads[4].wait()
    bgrad_v[...] = bsum_v[0:1, 0:CH]
    stores.append(pltpu.make_async_copy(bgrad_v, bgrad_hbm, store_sem.at[4]))
    stores[-1].start()
    for store in stores:
        store.wait()


def on_device(nc, volume, filters, bias, cotangent):
    ny = nc // 2
    chunk = HALF * nc
    dma = pltpu.SemaphoreType.DMA
    hbm = pl.BlockSpec(memory_space=pl.ANY)
    plane = (CH, VOX)
    sums = pl.pallas_call(
        functools.partial(kernel, nc, 1.0 / math.sqrt(nc * VOX)),
        out_shape=(
            jax.ShapeDtypeStruct(plane, BF16),
            jax.ShapeDtypeStruct(plane, BF16),
            jax.ShapeDtypeStruct((2 * CH, PADDED), F32),
            jax.ShapeDtypeStruct((8, 128), F32),
        ),
        in_specs=[hbm] * 4,
        out_specs=(hbm,) * 4,
        scratch_shapes=[
            pltpu.VMEM((TAPS, CH, 2 * CH), BF16),
            pltpu.VMEM((1, 2 * CH), BF16),
            pltpu.VMEM(plane, BF16),
            pltpu.VMEM((PADDED, 128), F32),
            pltpu.VMEM((2 * CH, PADDED), BF16),
            pltpu.VMEM((2, chunk, PADDED), BF16),
            pltpu.VMEM((4, 2 * CH, VOX), BF16),
            pltpu.VMEM((2, 4 * VIEWS, VOX), BF16),
            pltpu.VMEM((2, chunk, VOX), BF16),
            pltpu.VMEM((nc, CH, VOX), BF16),
            pltpu.VMEM(plane, BF16),
            pltpu.VMEM((2, chunk, VOX), BF16),
            pltpu.VMEM((2, chunk, PADDED), BF16),
            pltpu.VMEM((ny, 2 * CH, PADDED), BF16),
            pltpu.VMEM((8, 128), F32),
            pltpu.VMEM((nc, 8, 128), F32),
            pltpu.VMEM((2, PADDED, VOX), F32),
            pltpu.VMEM((4, CH, VOX), BF16),
            pltpu.VMEM((4, CH, VOX), BF16),
            pltpu.VMEM((4, CH, VOX), F32),
            pltpu.VMEM((3, CH, VOX), BF16),
            pltpu.VMEM((3, CH, VOX), BF16),
            pltpu.VMEM(plane, BF16),
            pltpu.VMEM(plane, BF16),
            pltpu.VMEM((2 * CH, PADDED), F32),
            pltpu.VMEM((8, 128), F32),
            dma((4,)), dma((5,)),
            dma((3,)), dma((3,)), dma((4,)), dma((4,)),
            dma((ny, 2, 2)), dma((ny, 2, 2)),
            dma((nc, 2)), dma((nc, 2)), dma((nc, 2)), dma((nc, 2)), dma((nc,)), dma((nc,)),
            dma((ny, 2, 2)), dma((ny, 2, 2)), dma((4,)), dma((4,)), dma((3,)), dma((3,)),
        ],
        compiler_params=pltpu.CompilerParams(
            collective_id=0, has_side_effects=True, vmem_limit_bytes=VMEM_LIMIT
        ),
    )(volume, filters, bias.reshape(1, 2 * CH), cotangent)
    output, data_grad, weight_grad, bias_grad = pl.pallas_call(
        finish,
        out_shape=(
            jax.ShapeDtypeStruct(plane, BF16),
            jax.ShapeDtypeStruct(plane, BF16),
            jax.ShapeDtypeStruct((TAPS, CH, 2 * CH), F32),
            jax.ShapeDtypeStruct((1, CH), F32),
        ),
        in_specs=[hbm] * 4,
        out_specs=(hbm,) * 4,
        scratch_shapes=[
            pltpu.VMEM(plane, BF16),
            pltpu.VMEM(plane, BF16),
            pltpu.VMEM((2 * CH, PADDED), F32),
            pltpu.VMEM((8, 128), F32),
            pltpu.VMEM((TAPS, CH, 2 * CH), F32),
            pltpu.VMEM((1, CH), F32),
            dma((5,)), dma((5,)),
        ],
        compiler_params=pltpu.CompilerParams(vmem_limit_bytes=VMEM_LIMIT),
    )(*sums)
    return output, data_grad, weight_grad, bias_grad.reshape(CH)


def solution(mesh):
    placed = (P("row", "col"), P(None, "row", "col"), P("col"), P("row", "col"))
    return jax.shard_map(
        functools.partial(on_device, mesh.shape["col"]),
        mesh=mesh,
        in_specs=placed,
        out_specs=(P("row", "col"), P("row", "col"), P(None, "row", "col"), P("row")),
        check_vma=False,
    )
```
